32 devices in a mesh: dp: 8 (over y, x, core), fsdp: 4 (over z).
Axes of the slice: x: 2, y: 2, z: 4, core: 2. Of those that a mesh axis runs over, the one named last changes fastest.
Arguments:
- student_tiles: bfloat16 [4096, 16, 256], P(('dp', 'fsdp')), may hold values from -6 to 6
- teacher_tiles: bfloat16 [4096, 16, 512], P(('dp', 'fsdp')), may hold values from -6 to 6
- send_list: int32 [8, 4, 128], P('dp', 'fsdp'), may hold values from -1 to 127, as said below
- clip_weight: float32 [4096], P(('dp', 'fsdp')), may hold values from 0.5 to 64, as said below
- kernel_dilated: bfloat16 [1792, 256], P('fsdp'), may hold values from -0.125 to 0.125
- kernel_mix: bfloat16 [256, 256], P('fsdp'), may hold values from -0.375 to 0.375
- kernel_down: bfloat16 [4096, 512], P('fsdp'), may hold values from -0.09375 to 0.09375
- kernel_proj: bfloat16 [512, 1024], P('fsdp'), may hold values from -0.25 to 0.25
- kernel_teacher: bfloat16 [16, 512, 1024], P(None, 'fsdp'), may hold values from -0.0625 to 0.0625
- alpha_one: float32 [256], replicated, may hold values from 0.5 to 2
- alpha_two: float32 [256], replicated, may hold values from 0.5 to 2
- alpha_three: float32 [256], replicated, may hold values from 0.5 to 2
- alpha_teacher: float32 [512], replicated, may hold values from 0.5 to 2
Outputs:
- student_latent: bfloat16 [4096, 2, 1024], P(('dp', 'fsdp'))
- grad_dilated: float32 [458752], P(('dp', 'fsdp'))
- grad_mix: float32 [65536], P(('dp', 'fsdp'))
- grad_down: float32 [2097152], P(('dp', 'fsdp'))
- grad_proj: float32 [524288], P(('dp', 'fsdp'))
The draws below stay inside these ranges and needn't reach their ends.
Inputs may be any that keep to these rules, and one draw needn't show every extreme that they name: `send_list`: entries d * 16 .. d * 16 + 15 of a device's list go to dp owner d. Each device's tiles 0 .. L - 1 appear exactly once and no other tile appears, for a count L of 16 to 128 drawn per device; on every device one owner receives 16 tiles, and some device has L = 128. `clip_weight`: positive weights.
All inputs are finite; a program needn't handle non-finite values.
Results may differ from the reference program's by a relative error of at most 0.0067.
Values may be sent and summed in bfloat16 or wider, within the bound.
No kernel may reach another device: no remote copies, remote signals or barrier semaphores. Data moves between devices by JAX's collectives and lax.ppermute only.
A program may use at most 128 MiB of HBM per device.

```python
import math
import jax
import jax.numpy as jnp
from jax import lax

CT = 512
DL = 1024
CS = 256
CSO = 512
KS = 16
STRIDE = 8
DILATED_TAPS = 7
UNIT_DILATION = 3
TILE_FRAMES = 16
TILE_DEV = 128
OUTF = 2
CAP = 16
TILES = 4096
N_DP = 8
N_FSDP = 4


def draw_send_list(key, part):
    devices_all = N_DP * N_FSDP
    key_length, key_full, key_first, key_shuffle = jax.random.split(key, 4)
    lengths = jax.random.randint(key_length, (devices_all,), CAP, TILE_DEV + 1)
    fullest = jax.random.randint(key_full, (), 0, devices_all)
    lengths = jnp.where(jnp.arange(devices_all) == fullest, TILE_DEV, lengths)
    first_owner = jax.random.randint(key_first, (devices_all,), 0, N_DP)
    shuffle = jax.vmap(lambda branch_key: jax.random.permutation(branch_key, TILE_DEV))(jax.random.split(key_shuffle, devices_all))
    position = jnp.arange(TILE_DEV)
    owner_index = position // CAP
    scores = jnp.where(owner_index[None, :] == first_owner[:, None], (position % CAP)[None, :], CAP + shuffle)
    ranking = jnp.argsort(jnp.argsort(scores, axis=1, stable=True), axis=1, stable=True)
    chosen = jnp.where(ranking < lengths[:, None], ranking, -1)
    return chosen.reshape(N_DP, N_FSDP, TILE_DEV).astype(jnp.int32)


def draw_clip_weight(key, part):
    devices_all = TILES // TILE_DEV
    base_key = jax.random.fold_in(key, 77)
    key_rank, key_rough = jax.random.split(base_key, 2)
    device_rank = jax.random.permutation(key_rank, devices_all).astype(jnp.float32)
    device_scale = 1.0 + 31.0 * jnp.power(jnp.float32(0.3), device_rank)
    rough = jnp.exp(jax.random.uniform(key_rough, (devices_all, TILE_DEV), jnp.float32, -0.693, 0.693))
    return (device_scale[:, None] * rough).reshape(-1).astype(jnp.float32)


def block_scale(stream_key, dims, cuts, low, largest):
    def one(dim, blocks):
        steps = jax.random.uniform(jax.random.fold_in(jax.random.fold_in(stream_key, 6), dim), (blocks,), jnp.float32, low / len(cuts), largest / len(cuts))
        return jnp.repeat(jnp.exp(steps), dims[dim] // blocks).reshape((-1,) + (1,) * (len(dims) - dim - 1))

    loudness = one(*cuts[0])
    for cut in cuts[1:]:
        loudness = loudness * one(*cut)
    return loudness


def centred(rng, dims, deviation, bound, cuts=(), held_as=jnp.bfloat16):
    values = jax.random.normal(rng, dims, jnp.float32) * deviation
    if len(cuts) > 0:
        values = block_scale(rng, dims, cuts, -0.22, 0.18) * values
    return jnp.clip(values, min=-bound, max=bound).astype(held_as)


def setup_inputs(seed: int = 0) -> dict:
    streams_of = jax.random.split(jax.random.key(seed), 14)
    student_tiles = centred(streams_of[0], (TILES, TILE_FRAMES, CS), 1.0, 6.0, ((0, 32),))
    teacher_tiles = centred(streams_of[1], (TILES, TILE_FRAMES, CT), 1.0, 6.0, ((0, 32),))
    send_list = draw_send_list(jax.random.fold_in(streams_of[13], 71), 0)
    clip_weight = draw_clip_weight(jax.random.fold_in(streams_of[13], 71), 0)
    kernel_dilated = centred(streams_of[4], (DILATED_TAPS * CS, CS), (DILATED_TAPS * CS) ** -0.5, 0.125, ((0, 4),))
    kernel_mix = centred(streams_of[5], (CS, CS), CS ** -0.5, 0.375, ((0, 4),))
    kernel_down = centred(streams_of[6], (KS * CS, CSO), (KS * CS) ** -0.5, 0.09375, ((0, 4),))
    kernel_proj = centred(streams_of[7], (CSO, DL), CSO ** -0.5, 0.25, ((0, 4),))
    kernel_teacher = centred(streams_of[8], (KS, CT, DL), (KS * CT) ** -0.5, 0.0625, ((1, 4),))
    alpha_one = jnp.clip(jnp.exp(jax.random.uniform(streams_of[9], (CS,), jnp.float32, math.log(0.5), math.log(2.0))), 0.5, 2.0)
    alpha_two = jnp.clip(jnp.exp(jax.random.uniform(streams_of[10], (CS,), jnp.float32, math.log(0.5), math.log(2.0))), 0.5, 2.0)
    alpha_three = jnp.clip(jnp.exp(jax.random.uniform(streams_of[11], (CS,), jnp.float32, math.log(0.5), math.log(2.0))), 0.5, 2.0)
    alpha_teacher = jnp.clip(jnp.exp(jax.random.uniform(streams_of[12], (CT,), jnp.float32, math.log(0.5), math.log(2.0))), 0.5, 2.0)
    return {"student_tiles": student_tiles, "teacher_tiles": teacher_tiles, "send_list": send_list, "clip_weight": clip_weight, "kernel_dilated": kernel_dilated, "kernel_mix": kernel_mix, "kernel_down": kernel_down, "kernel_proj": kernel_proj, "kernel_teacher": kernel_teacher, "alpha_one": alpha_one, "alpha_two": alpha_two, "alpha_three": alpha_three, "alpha_teacher": alpha_teacher}


def snake(values, alpha_vec):
    widened = values.astype(jnp.float32)
    return widened + jnp.square(jnp.sin(alpha_vec * widened)) / alpha_vec


def snake_slope(values, alpha_vec):
    return 1.0 + jnp.sin(2.0 * alpha_vec * values)


def unfold_strided(frames):
    tile_count = frames.shape[0]
    margin = (KS - STRIDE) // 2
    padded_frames = jnp.pad(frames, ((0, 0), (margin, margin), (0, 0)))
    windows = [padded_frames[:, STRIDE * offset:STRIDE * offset + KS, :].reshape(tile_count, -1) for offset in range(OUTF)]
    return jnp.stack(windows, axis=1)


def fold_strided(columns, channels):
    tile_count = columns.shape[0]
    margin = (KS - STRIDE) // 2
    padded_len = TILE_FRAMES + 2 * margin
    pieces = columns.reshape(tile_count, OUTF, KS, channels)
    folded = jnp.zeros((tile_count, padded_len, channels), jnp.float32)
    for offset in range(OUTF):
        folded = folded + jnp.pad(pieces[:, offset], ((0, 0), (STRIDE * offset, padded_len - KS - STRIDE * offset), (0, 0)))
    return folded[:, margin:margin + TILE_FRAMES, :]


def unfold_dilated(frames):
    tile_count = frames.shape[0]
    receptive_length = UNIT_DILATION * (DILATED_TAPS - 1) // 2
    padded_frames = jnp.pad(frames, ((0, 0), (receptive_length, receptive_length), (0, 0)))
    tap_offsets = [padded_frames[:, UNIT_DILATION * tap_position:UNIT_DILATION * tap_position + TILE_FRAMES, :] for tap_position in range(DILATED_TAPS)]
    return jnp.stack(tap_offsets, axis=2).reshape(tile_count * TILE_FRAMES, -1)


def teacher_forward(tiles, kernel_teacher, alpha_teacher):
    tile_count = tiles.shape[0]
    activated = snake(tiles, alpha_teacher).astype(jnp.bfloat16)
    columns = unfold_strided(activated).reshape(tile_count * OUTF, -1)
    latent = jnp.dot(columns, kernel_teacher.reshape(-1, DL), preferred_element_type=jnp.float32)
    return latent.reshape(tile_count, OUTF, DL).astype(jnp.bfloat16)


def student_step(tiles, target, weights, kernels, alphas):
    kernel_dilated, kernel_mix, kernel_down, kernel_proj = kernels
    alpha_one, alpha_two, alpha_three = alphas
    tile_count = tiles.shape[0]
    channels = tiles.shape[2]
    act_one = snake(tiles, alpha_one).astype(jnp.bfloat16)
    dilated = unfold_dilated(act_one)
    hidden = jnp.dot(dilated, kernel_dilated, preferred_element_type=jnp.float32)
    act_two = snake(hidden, alpha_two).astype(jnp.bfloat16)
    residual = tiles.reshape(tile_count * TILE_FRAMES, channels).astype(jnp.float32) + jnp.dot(act_two, kernel_mix, preferred_element_type=jnp.float32)
    act_three = snake(residual, alpha_three).astype(jnp.bfloat16).reshape(tile_count, TILE_FRAMES, channels)
    strided = unfold_strided(act_three).reshape(tile_count * OUTF, -1)
    student = jnp.dot(strided, kernel_down, preferred_element_type=jnp.float32).astype(jnp.bfloat16)
    predicted = jnp.dot(student, kernel_proj, preferred_element_type=jnp.float32)
    row_weight = jnp.repeat(weights.astype(jnp.float32), OUTF)[:, None]
    error = (row_weight * (predicted - target.reshape(tile_count * OUTF, DL).astype(jnp.float32)) / (tile_count * OUTF)).astype(jnp.bfloat16)
    grad_proj = jnp.dot(student.T, error, preferred_element_type=jnp.float32)
    back_student = jnp.dot(error, kernel_proj.T, preferred_element_type=jnp.float32).astype(jnp.bfloat16)
    grad_down = jnp.dot(strided.T, back_student, preferred_element_type=jnp.float32)
    back_columns = jnp.dot(back_student, kernel_down.T, preferred_element_type=jnp.float32).reshape(tile_count, OUTF, -1)
    back_three = fold_strided(back_columns, channels).reshape(tile_count * TILE_FRAMES, channels)
    back_residual = (back_three * snake_slope(residual, alpha_three)).astype(jnp.bfloat16)
    grad_mix = jnp.dot(act_two.T, back_residual, preferred_element_type=jnp.float32)
    back_hidden = (jnp.dot(back_residual, kernel_mix.T, preferred_element_type=jnp.float32) * snake_slope(hidden, alpha_two)).astype(jnp.bfloat16)
    grad_dilated = jnp.dot(dilated.T, back_hidden, preferred_element_type=jnp.float32)
    latent = predicted.astype(jnp.bfloat16).reshape(tile_count, OUTF, DL)
    return latent, (grad_dilated.reshape(-1), grad_mix.reshape(-1), grad_down.reshape(-1), grad_proj.reshape(-1))


def reference(student_tiles, teacher_tiles, send_list, clip_weight, kernel_dilated, kernel_mix, kernel_down, kernel_proj, kernel_teacher, alpha_one, alpha_two, alpha_three, alpha_teacher):
    devices_all = N_DP * N_FSDP
    routes = jnp.transpose(send_list.reshape(N_DP, N_FSDP, N_DP, CAP), (2, 1, 0, 3)).reshape(devices_all, TILE_DEV)
    source_dp = jnp.arange(TILE_DEV, dtype=jnp.int32) // CAP
    source_fsdp = jnp.arange(devices_all, dtype=jnp.int32) % N_FSDP
    anchor = ((source_dp[None, :] * N_FSDP + source_fsdp[:, None]) * TILE_DEV + jnp.maximum(routes, 0)).astype(jnp.int32)
    live_mask = routes >= 0
    weight_rows = clip_weight.reshape(devices_all, TILE_DEV)
    kernels = (kernel_dilated, kernel_mix, kernel_down, kernel_proj)
    alphas = (alpha_one, alpha_two, alpha_three)

    def per_device(totals, inputs):
        row_ids, used_rows, weights = inputs
        live_rows = used_rows[:, None, None]
        student_part = jnp.where(live_rows, jnp.take(student_tiles, row_ids, axis=0), jnp.zeros((), jnp.bfloat16))
        teacher_part = jnp.where(live_rows, jnp.take(teacher_tiles, row_ids, axis=0), jnp.zeros((), jnp.bfloat16))
        target = teacher_forward(teacher_part, kernel_teacher, alpha_teacher)
        latent, gradients = student_step(student_part, target, weights, kernels, alphas)
        return tuple(running + update for running, update in zip(totals, gradients)), latent

    zero_totals = tuple(jnp.zeros((kernel.size,), jnp.float32) for kernel in kernels)
    totals, latents = lax.scan(per_device, zero_totals, (anchor, live_mask, weight_rows))
    return (latents.reshape(TILES, OUTF, DL), totals[0], totals[1], totals[2], totals[3])
```

```python
import jax
import jax.numpy as jnp
from jax import lax
from jax.experimental import pallas as pl
from jax.experimental.pallas import tpu as pltpu
from jax.sharding import PartitionSpec as P

CT = 512
DL = 1024
CS = 256
CSO = 512
KS = 16
STRIDE = 8
DILATED_TAPS = 7
UNIT_DILATION = 3
TILE_FRAMES = 16
TILE_DEV = 128
OUTF = 2
MARGIN = (KS - STRIDE) // 2
ROWS = TILE_DEV * TILE_FRAMES
LATENTS = TILE_DEV * OUTF
N_FSDP = 4
QUARTER = CT // N_FSDP
GROUP = 16
SLABS = 4
F32 = jnp.float32
BF16 = jnp.bfloat16
VMEM_LIMIT = 48 * 1024 * 1024

PACK = {
    "dilated": DILATED_TAPS * CS // N_FSDP // SLABS,
    "mix": CS // N_FSDP // SLABS,
    "down": KS * CS // N_FSDP // SLABS,
    "proj": CSO // N_FSDP // SLABS,
}
PACK_COLS = {"dilated": 1, "mix": 1, "down": 2, "proj": 4}
PACK_ROWS = sum(PACK[name] * PACK_COLS[name] for name in PACK)

INV_PI = 0.3183098861837907
PI_PARTS = (3.125, 0.015625, 9.67502593994140625e-4, 1.509957990978376432e-7)
SIN_TERMS = (0.9999999765137553, -0.16666647593489264, 0.008332899222829617, -0.0001980086530702378, 2.5904300303557895e-06)
COS_TERMS = (0.999999953036273, -0.4999990494860951, 0.0416635772644784, -0.0013853657929132671, 2.3153011971441464e-05)


def _reduced(angle):
    turns = jnp.round(angle * INV_PI)
    for part in PI_PARTS:
        angle = angle - turns * part
    return angle


def _series(square, terms):
    total = square * terms[-1] + terms[-2]
    for term in terms[-3::-1]:
        total = total * square + term
    return total


def _snake(values, alpha, inverse):
    angle = _reduced(alpha * values)
    sine = angle * _series(angle * angle, SIN_TERMS)
    return values + sine * sine * inverse


def _snake_and_slope(values, alpha, inverse):
    angle = _reduced(alpha * values)
    square = angle * angle
    sine = angle * _series(square, SIN_TERMS)
    cosine = _series(square, COS_TERMS)
    return values + sine * sine * inverse, 1.0 + 2.0 * sine * cosine


def _dot(left, right):
    return jnp.dot(left, right, preferred_element_type=F32)


def _dot_nt(left, right):
    return lax.dot_general(left, right, (((1,), (1,)), ((), ())), preferred_element_type=F32)


def _dot_tn(left, right):
    return lax.dot_general(left, right, (((0,), (0,)), ((), ())), preferred_element_type=F32)


def _frame_major(block):
    count = GROUP * TILE_FRAMES
    target = lax.broadcasted_iota(jnp.int32, (count, count), 0)
    source = lax.broadcasted_iota(jnp.int32, (count, count), 1)
    wanted = (target % GROUP) * TILE_FRAMES + target // GROUP
    turn = jnp.where(source == wanted, 1.0, 0.0).astype(BF16)
    return _dot(turn, block)


def _teacher_act_kernel(place, tiles, alpha, *quarters):
    inverse = 1.0 / alpha[...]
    acted = _snake(_frame_major(tiles[...]), alpha[...], inverse).astype(BF16)
    del place
    for index, quarter in enumerate(quarters):
        part = acted[:, index * QUARTER : (index + 1) * QUARTER]
        quarter[...] = part.reshape(TILE_FRAMES, GROUP, QUARTER)


def _teacher_act(place, tiles, alpha):
    steps = TILE_DEV // GROUP
    shape = jax.ShapeDtypeStruct((TILE_FRAMES, TILE_DEV, QUARTER), BF16)
    return pl.pallas_call(
        _teacher_act_kernel,
        grid=(steps,),
        in_specs=[
            pl.BlockSpec(memory_space=pltpu.SMEM),
            pl.BlockSpec((GROUP * TILE_FRAMES, CT), lambda i: (i, 0)),
            pl.BlockSpec((1, CT), lambda i: (0, 0)),
        ],
        out_specs=[pl.BlockSpec((TILE_FRAMES, GROUP, QUARTER), lambda i: (0, i, 0))] * N_FSDP,
        out_shape=[shape] * N_FSDP,
        name="teacher_act",
        compiler_params=pltpu.CompilerParams(vmem_limit_bytes=VMEM_LIMIT),
        cost_estimate=pl.CostEstimate(flops=ROWS * CT * 512, bytes_accessed=4 * ROWS * CT, transcendentals=0),
    )(place, tiles.reshape(ROWS, CT), alpha.reshape(1, CT))


def _teacher_dot_kernel(frames, kernel, out):
    reach = STRIDE + MARGIN
    for offset in range(OUTF):
        first = max(0, STRIDE * offset - MARGIN)
        tap = first - (STRIDE * offset - MARGIN)
        wide = jnp.concatenate([frames[first + step] for step in range(reach)], axis=1)
        part = _dot(wide, kernel[tap * QUARTER : (tap + reach) * QUARTER, :])
        out[offset * TILE_DEV : (offset + 1) * TILE_DEV, :] = part.astype(out.dtype)


def _teacher_dot(frames, kernel, dtype):
    return pl.pallas_call(
        _teacher_dot_kernel,
        out_shape=jax.ShapeDtypeStruct((LATENTS, DL), dtype),
        name="teacher_dot",
        compiler_params=pltpu.CompilerParams(vmem_limit_bytes=VMEM_LIMIT),
        cost_estimate=pl.CostEstimate(
            flops=2 * LATENTS * 12 * QUARTER * DL, bytes_accessed=2 * KS * QUARTER * DL, transcendentals=0
        ),
    )(frames, kernel)


def _forward_kernel(
    place, tiles, own, other, alphas, routes,
    act_one, act_two, act_three, slope_two, slope_three, student, predicted, slots, mix, down, proj,
    dilated, held, sems,
):
    core = place[0]
    copies = []
    for half, (source, side) in enumerate(((own, core), (other, 1 - core))):
        row = 0
        for number, (name, target) in enumerate((("dilated", dilated), ("mix", mix), ("down", down), ("proj", proj))):
            rows, cols = PACK[name], PACK_COLS[name]
            view = target.reshape(N_FSDP, SLABS, rows, 2 * cols * 128)
            for col in range(cols):
                begin = pl.multiple_of(side * (cols * 128) + col * 128, 128)
                for slab in range(SLABS):
                    copies.append((number, pltpu.make_async_copy(
                        source.at[slab, :, pl.ds(row, rows), :],
                        view.at[:, slab, :, pl.ds(begin, 128)],
                        sems.at[number, half, slab * cols + col],
                    )))
                row += rows
    for _, copy in copies:
        copy.start()

    alpha_one, alpha_two, alpha_three = alphas[0:1, :], alphas[1:2, :], alphas[2:3, :]
    inverse_one, inverse_two, inverse_three = 1.0 / alpha_one, 1.0 / alpha_two, 1.0 / alpha_three
    for step in range(TILE_DEV // GROUP):
        turned = _frame_major(tiles[step * GROUP * TILE_FRAMES : (step + 1) * GROUP * TILE_FRAMES, :])
        shape = (TILE_FRAMES, GROUP, CS)
        held[:, step * GROUP : (step + 1) * GROUP, :] = turned.astype(BF16).reshape(shape)
        acted = _snake(turned, alpha_one, inverse_one).astype(BF16)
        act_one[:, step * GROUP : (step + 1) * GROUP, :] = acted.reshape(shape)

    def ready(wanted):
        for number, copy in copies:
            if number == wanted:
                copy.wait()

    ready(0)
    ready(1)
    half_taps = DILATED_TAPS // 2
    spans = []
    for frame in range(TILE_FRAMES):
        valid = [tap for tap in range(DILATED_TAPS) if 0 <= frame + UNIT_DILATION * (tap - half_taps) < TILE_FRAMES]
        span = (valid[0], valid[-1] + 1)
        if spans and spans[-1][2] == span:
            spans[-1][1] = frame + 1
        else:
            spans.append([frame, frame + 1, span])
    for start, stop, (low, high) in spans:
        wide = jnp.concatenate(
            [
                act_one[start + shift : stop + shift].reshape((stop - start) * TILE_DEV, CS)
                for shift in (UNIT_DILATION * (tap - half_taps) for tap in range(low, high))
            ],
            axis=1,
        )
        hidden = _dot(wide, dilated[low * CS : high * CS, :])
        acted, slope = _snake_and_slope(hidden, alpha_two, inverse_two)
        shape = (stop - start, TILE_DEV, CS)
        acted = acted.astype(BF16)
        act_two[start:stop] = acted.reshape(shape)
        slope_two[start:stop] = slope.reshape(shape)
        residual = held[start:stop].reshape((stop - start) * TILE_DEV, CS).astype(F32) + _dot(acted, mix[...])
        acted, slope = _snake_and_slope(residual, alpha_three, inverse_three)
        act_three[start:stop] = acted.astype(BF16).reshape(shape)
        slope_three[start:stop] = slope.reshape(shape)

    ready(2)
    reach = STRIDE + MARGIN
    for offset in range(OUTF):
        first = max(0, STRIDE * offset - MARGIN)
        tap = first - (STRIDE * offset - MARGIN)
        wide = jnp.concatenate([act_three[first + step] for step in range(reach)], axis=1)
        part = _dot(wide, down[tap * CS : (tap + reach) * CS, :])
        student[offset * TILE_DEV : (offset + 1) * TILE_DEV, :] = part.astype(BF16)
    ready(3)
    pick = jnp.where(
        routes[...] == lax.broadcasted_iota(jnp.int32, (TILE_DEV, TILE_DEV), 1), 1.0, 0.0
    ).astype(BF16)
    for offset in range(OUTF):
        rows = slice(offset * TILE_DEV, (offset + 1) * TILE_DEV)
        part = _dot(student[rows, :], proj[...])
        predicted[rows, :] = part
        slots[:, offset * DL : (offset + 1) * DL] = _dot(pick, part.astype(BF16)).astype(BF16)


def _forward(place, tiles, own, other, alphas, routes):
    frames = (TILE_FRAMES, TILE_DEV, CS)
    whole = pl.BlockSpec(memory_space=pltpu.VMEM)
    return pl.pallas_call(
        _forward_kernel,
        in_specs=[
            pl.BlockSpec(memory_space=pltpu.SMEM),
            whole,
            pl.BlockSpec(memory_space=pl.ANY),
            pl.BlockSpec(memory_space=pl.ANY),
            whole,
            whole,
        ],
        out_specs=[whole] * 11,
        out_shape=[
            jax.ShapeDtypeStruct(frames, BF16),
            jax.ShapeDtypeStruct(frames, BF16),
            jax.ShapeDtypeStruct(frames, BF16),
            jax.ShapeDtypeStruct(frames, F32),
            jax.ShapeDtypeStruct(frames, F32),
            jax.ShapeDtypeStruct((LATENTS, CSO), BF16),
            jax.ShapeDtypeStruct((LATENTS, DL), F32),
            jax.ShapeDtypeStruct((TILE_DEV, OUTF * DL), BF16),
            jax.ShapeDtypeStruct((CS, CS), BF16),
            jax.ShapeDtypeStruct((KS * CS, CSO), BF16),
            jax.ShapeDtypeStruct((CSO, DL), BF16),
        ],
        scratch_shapes=[
            pltpu.VMEM((DILATED_TAPS * CS, CS), BF16),
            pltpu.VMEM(frames, BF16),
            pltpu.SemaphoreType.DMA((4, 2, 16)),
        ],
        name="student_forward",
        compiler_params=pltpu.CompilerParams(vmem_limit_bytes=VMEM_LIMIT),
        cost_estimate=pl.CostEstimate(flops=4_000_000_000, bytes_accessed=30_000_000, transcendentals=0),
    )(place, tiles.reshape(ROWS, CS), own, other, alphas, routes)


def _stacked(values, columns):
    return jnp.concatenate(
        [values[:, start : start + columns] for start in range(0, values.shape[1], columns)], axis=0
    )


def _strided_kernel(
    place, target_own, target_one, target_two, target_three, predicted, weights, student, proj, act_three,
    back_student, send_a, send_b, keep_a, keep_b, error, grad_proj, padded,
):
    me = place[1]
    weight = weights[...] * (1.0 / LATENTS)
    for offset in range(OUTF):
        rows = slice(offset * TILE_DEV, (offset + 1) * TILE_DEV)
        target = target_own[rows, :] + target_one[rows, :].astype(F32)
        target += target_two[rows, :].astype(F32)
        target += target_three[rows, :].astype(F32)
        target = target.astype(BF16).astype(F32)
        error[rows, :] = (weight * (predicted[rows, :] - target)).astype(BF16)
    back = _dot_nt(error[...], proj[...]).astype(BF16)
    back_student[...] = back
    grad_proj[...] = _dot_tn(student[...], error[...])

    blank = jnp.zeros((MARGIN, TILE_DEV, CS), BF16)
    padded[0:MARGIN] = blank
    padded[MARGIN : MARGIN + TILE_FRAMES] = act_three[...]
    padded[MARGIN + TILE_FRAMES :] = blank

    for pair in range(KS):
        tap = (me // 2) ^ pair
        wide = jnp.concatenate([padded[tap + STRIDE * offset] for offset in range(OUTF)], axis=0)
        grad = _dot_tn(wide, back)
        outs = (send_a, send_b) if (pair // 2) % 2 else (keep_a, keep_b)
        slot = (pair // 4) * 4 + (pair % 2) * 2
        for half in range(2):
            spot = slot + (half ^ (me % 2))
            part = grad[half * 128 : (half + 1) * 128, :]
            share = grad_proj[pl.ds(pl.multiple_of((tap * 2 + half) * 16, 16), 16), :]
            for index, out in enumerate(outs):
                out[spot, 0:128, :] = part[:, index * 256 : (index + 1) * 256].astype(out.dtype)
                out[spot, 128:160, :] = _stacked(share[:, index * 512 : (index + 1) * 512], 256).astype(out.dtype)


def _strided(place, targets, predicted, weights, student, proj, act_three):
    whole = pl.BlockSpec(memory_space=pltpu.VMEM)
    half = (16, 160, 256)
    return pl.pallas_call(
        _strided_kernel,
        in_specs=[pl.BlockSpec(memory_space=pltpu.SMEM)] + [whole] * 9,
        out_specs=[whole] * 5,
        out_shape=[
            jax.ShapeDtypeStruct((LATENTS, CSO), BF16),
            jax.ShapeDtypeStruct(half, BF16),
            jax.ShapeDtypeStruct(half, BF16),
            jax.ShapeDtypeStruct(half, F32),
            jax.ShapeDtypeStruct(half, F32),
        ],
        scratch_shapes=[
            pltpu.VMEM((LATENTS, DL), BF16),
            pltpu.VMEM((CSO, DL), F32),
            pltpu.VMEM((TILE_FRAMES + 2 * MARGIN, TILE_DEV, CS), BF16),
        ],
        name="strided_backward",
        compiler_params=pltpu.CompilerParams(vmem_limit_bytes=VMEM_LIMIT),
        cost_estimate=pl.CostEstimate(flops=2_000_000_000, bytes_accessed=16_000_000, transcendentals=0),
    )(place, *targets, predicted, weights, student, proj, act_three)


def _residual_kernel(
    place, back_student, down, mix, act_one, act_two, slope_two, slope_three,
    send, keep, back_three, back_residual, back_hidden, grad_dilated, grad_mix,
):
    me = place[1]
    back = back_student[...]
    for tap in range(KS):
        part = _dot_nt(back, down[tap * CS : (tap + 1) * CS, :])
        for offset in range(OUTF):
            frame = STRIDE * offset - MARGIN + tap
            if 0 <= frame < TILE_FRAMES:
                piece = part[offset * TILE_DEV : (offset + 1) * TILE_DEV, :]
                if offset == 0 and frame >= MARGIN:
                    back_three[frame] += piece
                else:
                    back_three[frame] = piece
    for frame in range(0, TILE_FRAMES, 2):
        rows = slice(frame * TILE_DEV, (frame + 2) * TILE_DEV)
        shape = (2 * TILE_DEV, CS)
        share = back_three[frame : frame + 2].reshape(shape) * slope_three[frame : frame + 2].reshape(shape)
        share = share.astype(BF16)
        back_residual[rows, :] = share
        share = _dot_nt(share, mix[...]) * slope_two[frame : frame + 2].reshape(shape)
        back_hidden[rows, :] = share.astype(BF16)
    grad_mix[...] = _dot_tn(act_two[...].reshape(ROWS, CS), back_residual[...])
    half_taps = DILATED_TAPS // 2
    for tap in range(DILATED_TAPS):
        shift = UNIT_DILATION * (tap - half_taps)
        first, last = max(0, -shift), min(TILE_FRAMES, TILE_FRAMES - shift)
        rows = (last - first) * TILE_DEV
        grad_dilated[tap * CS : (tap + 1) * CS, :] = _dot_tn(
            act_one[first + shift : last + shift].reshape(rows, CS), back_hidden[first * TILE_DEV : last * TILE_DEV, :]
        )
    for place_index in range(32):
        chunk = me ^ place_index
        part = jnp.concatenate(
            [
                grad_dilated[pl.ds(pl.multiple_of(chunk * 56, 8), 56), :],
                grad_mix[pl.ds(pl.multiple_of(chunk * 8, 8), 8), :],
            ],
            axis=0,
        )
        out = send if (place_index // 4) % 2 else keep
        out[(place_index // 8) * 4 + place_index % 4] = part.astype(out.dtype)


def _residual(place, back_student, down, mix, act_one, act_two, slope_two, slope_three):
    whole = pl.BlockSpec(memory_space=pltpu.VMEM)
    half = (16, 64, 256)
    return pl.pallas_call(
        _residual_kernel,
        in_specs=[pl.BlockSpec(memory_space=pltpu.SMEM)] + [whole] * 7,
        out_specs=[whole] * 2,
        out_shape=[jax.ShapeDtypeStruct(half, BF16), jax.ShapeDtypeStruct(half, F32)],
        scratch_shapes=[
            pltpu.VMEM((TILE_FRAMES, TILE_DEV, CS), F32),
            pltpu.VMEM((ROWS, CS), BF16),
            pltpu.VMEM((ROWS, CS), BF16),
            pltpu.VMEM((DILATED_TAPS * CS, CS), F32),
            pltpu.VMEM((CS, CS), F32),
        ],
        name="residual_backward",
        compiler_params=pltpu.CompilerParams(vmem_limit_bytes=VMEM_LIMIT),
        cost_estimate=pl.CostEstimate(flops=3_500_000_000, bytes_accessed=16_000_000, transcendentals=0),
    )(place, back_student, down, mix, act_one, act_two, slope_two, slope_three)


def _swap(values, axis, bit):
    return lax.ppermute(values, axis, [(i, i ^ bit) for i in range(lax.axis_size(axis))])


def _share_of(kernel, slab, side):
    rows, cols = kernel.shape[0] // SLABS, kernel.shape[1] // 2
    part = lax.dynamic_slice(kernel, (slab * rows, side * cols), (rows, cols))
    return _stacked(part, 128)


def on_device(
    student_tiles,
    teacher_tiles,
    send_list,
    clip_weight,
    kernel_dilated,
    kernel_mix,
    kernel_down,
    kernel_proj,
    kernel_teacher,
    alpha_one,
    alpha_two,
    alpha_three,
    alpha_teacher,
):
    n_dp = lax.axis_size("dp")
    d, f = lax.axis_index("dp"), lax.axis_index("fsdp")
    core, slab = d % 2, (d // 2) % SLABS
    halving = n_dp == 8
    me = d * N_FSDP + f if halving else jnp.int32(0)
    place = jnp.stack([core, me]).astype(jnp.int32)

    routes = send_list.reshape(-1)
    cap = TILE_DEV // n_dp
    all_weights = lax.all_gather(clip_weight, "dp", axis=0, tiled=False)
    slot_weights = lax.dynamic_slice(all_weights, (0, d * cap), (n_dp, cap)).reshape(-1)
    hits = routes[:, None] == jnp.arange(TILE_DEV, dtype=jnp.int32)[None, :]
    weights = jnp.sum(jnp.where(hits, slot_weights[:, None], 0.0), axis=0)[:, None]

    quarters = jnp.stack(_teacher_act(place, teacher_tiles, alpha_teacher))
    flat_teacher = kernel_teacher.reshape(KS * QUARTER, DL)
    partials = []
    for bit in range(1, N_FSDP):
        sent = _swap(lax.dynamic_index_in_dim(quarters, f ^ bit, 0, keepdims=False), "fsdp", bit)
        partials.append(_swap(_teacher_dot(sent, flat_teacher, BF16), "fsdp", bit))
    own_partial = _teacher_dot(lax.dynamic_index_in_dim(quarters, f, 0, keepdims=False), flat_teacher, F32)

    packed = jnp.concatenate(
        [_share_of(k, slab, core) for k in (kernel_dilated, kernel_mix, kernel_down, kernel_proj)], axis=0
    )
    packed = lax.all_gather(packed, "fsdp", axis=0, tiled=False)
    planes = [[base + 2 * i + c for i in range(SLABS)] for base in range(0, n_dp, 8) for c in range(2)]
    own = lax.all_gather(packed, "dp", axis=0, tiled=False, axis_index_groups=planes)
    other = _swap(own, "dp", 1)

    alphas = jnp.stack([alpha_one, alpha_two, alpha_three])
    (
        act_one, act_two, act_three, slope_two, slope_three, student, predicted, slots, mix, down, proj,
    ) = _forward(place, student_tiles, own, other, alphas, routes[:, None])
    latent = lax.all_to_all(slots, "dp", split_axis=0, concat_axis=0, tiled=True).reshape(TILE_DEV, OUTF, DL)

    back_student, send_a, send_b, keep_a, keep_b = _strided(
        place, (own_partial, *partials), predicted, weights, student, proj, act_three
    )
    send_s, keep_s = _residual(place, back_student, down, mix, act_one, act_two, slope_two, slope_three)

    if halving:
        def halve(keep, received, axis_bit):
            total = keep + received.astype(F32)
            return total[0], total[1].astype(BF16), axis_bit

        def reduce_plane(send, keep, order):
            rows = keep.shape[1]
            keep = keep.reshape(2, 2, N_FSDP, rows, 256)
            received = _swap(send, "dp", 1).reshape(keep.shape)
            if order == "xy":
                keep, received = jnp.swapaxes(keep, 0, 1), jnp.swapaxes(received, 0, 1)
            bits = (2, 4) if order == "xy" else (4, 2)
            for bit in bits:
                keep, out, _ = halve(keep, received, bit)
                received = _swap(out, "dp", bit)
            return keep + received.astype(F32)

        parts = [
            reduce_plane(send_a, keep_a, "xy"),
            reduce_plane(send_b, keep_b, "yx"),
            reduce_plane(send_s, keep_s, "xy"),
        ]
        finals = []
        for part in parts:
            total = part[0]
            for bit in range(1, N_FSDP):
                total = total + _swap(part[bit].astype(BF16), "fsdp", bit).astype(F32)
            finals.append(total)
        part_a, part_b, part_s = finals
        grad_down = jnp.concatenate([part_a[:128], part_b[:128]], axis=1).reshape(-1)
        grad_proj = jnp.concatenate(
            [part_a[128:144], part_a[144:160], part_b[128:144], part_b[144:160]], axis=1
        ).reshape(-1)
        grad_dilated, grad_mix = part_s[:56].reshape(-1), part_s[56:].reshape(-1)
    else:
        def joined(send, keep):
            rows = keep.shape[1]
            both = jnp.stack([keep.reshape(4, 4, rows, 256), send.astype(F32).reshape(4, 4, rows, 256)], axis=1)
            return both.reshape(32, rows, 256)

        part_a, part_b, part_s = joined(send_a, keep_a), joined(send_b, keep_b), joined(send_s, keep_s)

        def scattered(values):
            return lax.psum_scatter(values.reshape(-1), ("dp", "fsdp"), scatter_dimension=0, tiled=True)

        grad_down = scattered(jnp.concatenate([part_a[:, :128], part_b[:, :128]], axis=2))
        grad_proj = scattered(
            jnp.concatenate([part_a[:, 128:144], part_a[:, 144:], part_b[:, 128:144], part_b[:, 144:]], axis=2)
        )
        grad_dilated, grad_mix = scattered(part_s[:, :56]), scattered(part_s[:, 56:])
    return latent, grad_dilated, grad_mix, grad_down, grad_proj


def solution(mesh):
    placed = (
        P(("dp", "fsdp"), None, None),
        P(("dp", "fsdp"), None, None),
        P("dp", "fsdp", None),
        P(("dp", "fsdp")),
        P("fsdp", None),
        P("fsdp", None),
        P("fsdp", None),
        P("fsdp", None),
        P(None, "fsdp", None),
        P(),
        P(),
        P(),
        P(),
    )
    return jax.shard_map(
        on_device,
        mesh=mesh,
        in_specs=placed,
        out_specs=(
            P(("dp", "fsdp"), None, None),
            P(("dp", "fsdp")),
            P(("dp", "fsdp")),
            P(("dp", "fsdp")),
            P(("dp", "fsdp")),
        ),
        check_vma=False,
    )
```

```python
import jax
import jax.numpy as jnp
from jax import lax
from jax.experimental import pallas as pl
from jax.experimental.pallas import tpu as pltpu
from jax.sharding import PartitionSpec as P

CT = 512
DL = 1024
CS = 256
CSO = 512
KS = 16
STRIDE = 8
DILATED_TAPS = 7
UNIT_DILATION = 3
TILE_FRAMES = 16
TILE_DEV = 128
CHUNKS = 32
OUTF = 2
MARGIN = (KS - STRIDE) // 2
SHARE = TILE_DEV // 8
WINDOW_ROWS = 2 * OUTF * TILE_DEV
WEIGHT_ROW = WINDOW_ROWS + OUTF * DL // CS * SHARE
ROWS = TILE_DEV * TILE_FRAMES
LATENTS = TILE_DEV * OUTF
N_FSDP = 4
QUARTER = CT // N_FSDP
GROUP = 16
SLABS = 4
F32 = jnp.float32
BF16 = jnp.bfloat16
VMEM_LIMIT = 48 * 1024 * 1024
COST = pl.CostEstimate(flops=1000, bytes_accessed=1000, transcendentals=0)

PACK = {
    "dilated": DILATED_TAPS * CS // N_FSDP // SLABS,
    "mix": CS // N_FSDP // SLABS,
    "down": KS * CS // N_FSDP // SLABS,
    "proj": CSO // N_FSDP // SLABS,
}
PACK_COLS = {"dilated": 1, "mix": 1, "down": 2, "proj": 4}
PACK_ROWS = sum(PACK[name] * PACK_COLS[name] for name in PACK)

INV_PI = 0.3183098861837907
PI_PARTS = (3.125, 0.015625, 9.67502593994140625e-4, 1.509957990978376432e-7)
SIN_TERMS = (0.9999999765137553, -0.16666647593489264, 0.008332899222829617, -0.0001980086530702378, 2.5904300303557895e-06)
COS_TERMS = (0.999999953036273, -0.4999990494860951, 0.0416635772644784, -0.0013853657929132671, 2.3153011971441464e-05)


def _reduced(angle):
    turns = jnp.round(angle * INV_PI)
    for part in PI_PARTS:
        angle = angle - turns * part
    return angle


def _series(square, terms):
    total = square * terms[-1] + terms[-2]
    for term in terms[-3::-1]:
        total = total * square + term
    return total


def _snake(values, alpha, inverse):
    angle = _reduced(alpha * values)
    sine = angle * _series(angle * angle, SIN_TERMS)
    return values + sine * sine * inverse


def _snake_and_slope(values, alpha, inverse):
    angle = _reduced(alpha * values)
    square = angle * angle
    sine = angle * _series(square, SIN_TERMS)
    cosine = _series(square, COS_TERMS)
    return values + sine * sine * inverse, 1.0 + 2.0 * sine * cosine


def _dot(left, right):
    return jnp.dot(left, right, preferred_element_type=F32)


def _dot_nt(left, right):
    return lax.dot_general(left, right, (((1,), (1,)), ((), ())), preferred_element_type=F32)


def _dot_tn(left, right):
    return lax.dot_general(left, right, (((0,), (0,)), ((), ())), preferred_element_type=F32)


def _turn():
    count = GROUP * TILE_FRAMES
    target = lax.broadcasted_iota(jnp.int32, (count, count), 0)
    source = lax.broadcasted_iota(jnp.int32, (count, count), 1)
    wanted = (target % GROUP) * TILE_FRAMES + target // GROUP
    return jnp.where(source == wanted, 1.0, 0.0).astype(BF16)


def _teacher_act_kernel(place, tiles, alpha, keep, send):
    fsdp = place[2]
    turn = _turn()
    for out, first in ((keep, fsdp), (send, fsdp ^ 1)):
        for index in range(2):
            lanes = pl.ds(pl.multiple_of((first ^ (2 * index)) * QUARTER, QUARTER), QUARTER)
            scale = alpha[:, lanes]
            acted = _snake(_dot(turn, tiles[:, lanes]), scale, 1.0 / scale).astype(BF16)
            out[index] = acted.reshape(TILE_FRAMES, GROUP, QUARTER)


def _teacher_act(place, tiles, alpha):
    steps = TILE_DEV // GROUP
    shape = jax.ShapeDtypeStruct((2, TILE_FRAMES, TILE_DEV, QUARTER), BF16)
    return pl.pallas_call(
        _teacher_act_kernel,
        grid=(steps,),
        in_specs=[
            pl.BlockSpec(memory_space=pltpu.SMEM),
            pl.BlockSpec((GROUP * TILE_FRAMES, CT), lambda i: (i, 0)),
            pl.BlockSpec((1, CT), lambda i: (0, 0)),
        ],
        out_specs=[pl.BlockSpec((2, TILE_FRAMES, GROUP, QUARTER), lambda i: (0, 0, i, 0))] * 2,
        out_shape=[shape] * 2,
        name="teacher_act",
        compiler_params=pltpu.CompilerParams(vmem_limit_bytes=VMEM_LIMIT),
        cost_estimate=COST,
    )(place, tiles.reshape(ROWS, CT), alpha.reshape(1, CT))


def _pack_kernel(place, dilated, mix, down, proj, teacher, packed, columns, sems):
    core, slab = place[0], place[3]
    copies = []
    row = 0
    for name, source in (("dilated", dilated), ("mix", mix), ("down", down), ("proj", proj)):
        rows = PACK[name]
        for block in range(PACK_COLS[name]):
            begin = pl.multiple_of((core * PACK_COLS[name] + block) * 128, 128)
            copies.append(pltpu.make_async_copy(
                source.at[pl.ds(pl.multiple_of(slab * rows, 16), rows), pl.ds(begin, 128)],
                packed.at[pl.ds(row, rows), :],
                sems.at[len(copies)],
            ))
            row += rows
    begin = pl.multiple_of((core * SLABS + slab) * 128, 128)
    copies.append(pltpu.make_async_copy(teacher.at[:, pl.ds(begin, 128)], columns, sems.at[len(copies)]))
    for copy in copies:
        copy.start()
    for copy in copies:
        copy.wait()


def _pack(place, *kernels):
    anywhere = pl.BlockSpec(memory_space=pl.ANY)
    return pl.pallas_call(
        _pack_kernel,
        in_specs=[pl.BlockSpec(memory_space=pltpu.SMEM)] + [anywhere] * 5,
        out_specs=[pl.BlockSpec(memory_space=pltpu.VMEM)] * 2,
        out_shape=[
            jax.ShapeDtypeStruct((PACK_ROWS, 128), BF16),
            jax.ShapeDtypeStruct((KS * QUARTER, 128), BF16),
        ],
        scratch_shapes=[pltpu.SemaphoreType.DMA((9,))],
        name="pack_kernels",
        cost_estimate=COST,
    )(place, *kernels)


def _early(parts, slab):
    return parts[slab // 2].at[slab % 2]


def _late(parts, slab):
    return parts[2 + slab % 2].at[slab // 2]


def _windows(mine, theirs, quarter, offset):
    first = max(0, STRIDE * offset - MARGIN)
    wide = [
        jnp.concatenate([tiles[quarter, first + step] for step in range(STRIDE + MARGIN)], axis=1)
        for tiles in (mine, theirs)
    ]
    return jnp.concatenate(wide, axis=0), first - (STRIDE * offset - MARGIN)


def _teacher_near_kernel(mine, theirs, kernel, out):
    for offset in range(OUTF):
        wide, tap = _windows(mine, theirs, 0, offset)
        part = _dot(wide, kernel[tap * QUARTER : (tap + STRIDE + MARGIN) * QUARTER, :])
        for device in range(2):
            start = device * LATENTS + offset * TILE_DEV
            out[start : start + TILE_DEV, :] = part[device * TILE_DEV : (device + 1) * TILE_DEV, :]


def _teacher_near(mine, theirs, kernel):
    return pl.pallas_call(
        _teacher_near_kernel,
        out_shape=jax.ShapeDtypeStruct((2 * LATENTS, DL), F32),
        name="teacher_near",
        compiler_params=pltpu.CompilerParams(vmem_limit_bytes=VMEM_LIMIT),
        cost_estimate=COST,
    )(mine, theirs, kernel)


def _teacher_far_kernel(place, near, mine, theirs, *refs):
    own, other, (keep, send) = refs[:4], refs[4:8], refs[8:]
    core, plane = place[0], place[3]
    taps = KS // 2 * QUARTER
    skipped = MARGIN * QUARTER
    for offset in range(OUTF):
        wide, tap = _windows(mine, theirs, 1, offset)
        for side, source in enumerate((own, other)):
            for pair in range(0, SLABS, 2):
                columns = []
                for slab in (pair, pair + 1):
                    early, late = _early(source, slab)[...], _late(source, slab)[...]
                    if tap:
                        columns.append(jnp.concatenate([early[skipped:], late], axis=0))
                    else:
                        columns.append(jnp.concatenate([early, late[: taps - skipped]], axis=0))
                part = _dot(wide, jnp.concatenate(columns, axis=1))
                for index, slab in enumerate((pair, pair + 1)):
                    block = (core ^ side) * SLABS + (plane ^ slab)
                    lanes = pl.ds(pl.multiple_of(block * 128, 128), 128)
                    for device, out in enumerate((keep, send)):
                        piece = part[device * TILE_DEV : (device + 1) * TILE_DEV, index * 128 : (index + 1) * 128]
                        start = device * LATENTS + offset * TILE_DEV
                        piece += near[start : start + TILE_DEV, lanes]
                        out[offset * TILE_DEV : (offset + 1) * TILE_DEV, lanes] = piece.astype(out.dtype)


def _teacher_far(place, near, mine, theirs, own, other):
    whole = pl.BlockSpec(memory_space=pltpu.VMEM)
    return pl.pallas_call(
        _teacher_far_kernel,
        in_specs=[pl.BlockSpec(memory_space=pltpu.SMEM)] + [whole] * 11,
        out_specs=[whole] * 2,
        out_shape=[jax.ShapeDtypeStruct((LATENTS, DL), F32), jax.ShapeDtypeStruct((LATENTS, DL), BF16)],
        name="teacher_far",
        compiler_params=pltpu.CompilerParams(vmem_limit_bytes=VMEM_LIMIT),
        cost_estimate=COST,
    )(place, near, mine, theirs, *own, *other)


def _lanes(blocks, rows):
    return jnp.concatenate([blocks[index, rows, :] for index in range(blocks.shape[0])], axis=1)


def _forward_kernel(
    place, tiles, own_a, own_b, own_c, own_d, other_a, other_b, other_c, other_d,
    near_dilated, near_mix, near_down, near_proj, alphas, routes, weights,
    act_one, act_two, act_three, slope_two, slope_three, student, predicted, mix, down, proj, parcel,
    dilated, held,
):
    own, other = (own_a, own_b, own_c, own_d), (other_a, other_b, other_c, other_d)
    core, fsdp, plane = place[0], place[2], place[3]

    def rows_of(quarter, slab, share):
        return pl.ds(pl.multiple_of(quarter * (SLABS * share) + slab * share, 16), share)

    kinds = ((near_dilated, dilated), (near_mix, mix), (near_down, down), (near_proj, proj))
    for name, (source, target) in zip(PACK, kinds):
        rows = pl.ds(pl.multiple_of(fsdp * (SLABS * PACK[name]), 16), SLABS * PACK[name])
        for block in range(target.shape[0]):
            target[block, rows, :] = source[:, block * 128 : (block + 1) * 128]
    for flip, pieces in enumerate((own, other)):
        side = core ^ flip
        for slab in range(SLABS):
            for bit in range(1, N_FSDP):
                early, late = _early(pieces, slab).at[bit - 1], _late(pieces, slab).at[bit - 1]
                quarter, chip = fsdp ^ bit, plane ^ slab
                dilated[side, rows_of(quarter, chip, PACK["dilated"]), :] = early[0:112, :]
                mix[side, rows_of(quarter, chip, PACK["mix"]), :] = early[112:128, :]
                rows = rows_of(quarter, chip, PACK["down"])
                down[side * 2, rows, :] = early[128:384, :]
                down[side * 2 + 1, rows, :] = late[0:256, :]
                rows = rows_of(quarter, chip, PACK["proj"])
                for block in range(4):
                    proj[side * 4 + block, rows, :] = late[256 + block * 32 : 288 + block * 32, :]

    alpha_one, alpha_two, alpha_three = alphas[0:1, :], alphas[1:2, :], alphas[2:3, :]
    inverse_one, inverse_two, inverse_three = 1.0 / alpha_one, 1.0 / alpha_two, 1.0 / alpha_three
    turn = _turn()
    for step in range(TILE_DEV // GROUP):
        turned = _dot(turn, tiles[step * GROUP * TILE_FRAMES : (step + 1) * GROUP * TILE_FRAMES, :])
        shape = (TILE_FRAMES, GROUP, CS)
        held[:, step * GROUP : (step + 1) * GROUP, :] = turned.astype(BF16).reshape(shape)
        acted = _snake(turned, alpha_one, inverse_one).astype(BF16)
        act_one[:, step * GROUP : (step + 1) * GROUP, :] = acted.reshape(shape)

    half_taps = DILATED_TAPS // 2
    spans = []
    for frame in range(TILE_FRAMES):
        valid = [tap for tap in range(DILATED_TAPS) if 0 <= frame + UNIT_DILATION * (tap - half_taps) < TILE_FRAMES]
        span = (valid[0], valid[-1] + 1)
        if spans and spans[-1][2] == span:
            spans[-1][1] = frame + 1
        else:
            spans.append([frame, frame + 1, span])
    for start, stop, (low, high) in spans:
        wide = jnp.concatenate(
            [
                act_one[start + shift : stop + shift].reshape((stop - start) * TILE_DEV, CS)
                for shift in (UNIT_DILATION * (tap - half_taps) for tap in range(low, high))
            ],
            axis=1,
        )
        hidden = _dot(wide, _lanes(dilated, slice(low * CS, high * CS)))
        acted, slope = _snake_and_slope(hidden, alpha_two, inverse_two)
        shape = (stop - start, TILE_DEV, CS)
        acted = acted.astype(BF16)
        act_two[start:stop] = acted.reshape(shape)
        slope_two[start:stop] = slope.reshape(shape)
        residual = held[start:stop].reshape((stop - start) * TILE_DEV, CS).astype(F32) + _dot(acted, _lanes(mix, slice(None)))
        acted, slope = _snake_and_slope(residual, alpha_three, inverse_three)
        act_three[start:stop] = acted.astype(BF16).reshape(shape)
        slope_three[start:stop] = slope.reshape(shape)

    reach = STRIDE + MARGIN
    for offset in range(OUTF):
        first = max(0, STRIDE * offset - MARGIN)
        tap = first - (STRIDE * offset - MARGIN)
        wide = jnp.concatenate([act_three[first + step] for step in range(reach)], axis=1)
        part = _dot(wide, _lanes(down, slice(tap * CS, (tap + reach) * CS)))
        student[offset * TILE_DEV : (offset + 1) * TILE_DEV, :] = part.astype(BF16)
    pick = jnp.where(
        routes[...] == lax.broadcasted_iota(jnp.int32, (TILE_DEV, TILE_DEV), 1), 1.0, 0.0
    ).astype(BF16)
    for offset in range(OUTF):
        rows = slice(offset * TILE_DEV, (offset + 1) * TILE_DEV)
        part = _dot(student[rows, :], _lanes(proj, slice(None)))
        predicted[rows, :] = part
        picked = _dot(pick, part.astype(BF16)).astype(BF16)
        for block in range(DL // CS):
            row = WINDOW_ROWS + (offset * (DL // CS) + block) * SHARE
            for owner in range(8):
                parcel[owner, row : row + SHARE, :] = picked[
                    owner * SHARE : (owner + 1) * SHARE, block * CS : (block + 1) * CS
                ]
    first = weights[...].astype(BF16).astype(F32)
    second = (weights[...] - first).astype(BF16).astype(F32)
    third = weights[...] - first - second
    lane = lax.broadcasted_iota(jnp.int32, (TILE_DEV, CS), 1)
    split = jnp.where(lane == 0, first, jnp.where(lane == 1, second, jnp.where(lane == 2, third, 0.0))).astype(BF16)
    for owner in range(8):
        parcel[owner, WEIGHT_ROW:, :] = split[owner * SHARE : (owner + 1) * SHARE, :]
    for tap in range(KS):
        for offset in range(OUTF):
            frame = STRIDE * offset - MARGIN + tap
            row = (tap % 2 * OUTF + offset) * TILE_DEV
            if 0 <= frame < TILE_FRAMES:
                parcel[tap // 2, row : row + TILE_DEV, :] = act_three[frame]
            else:
                parcel[tap // 2, row : row + TILE_DEV, :] = jnp.zeros((TILE_DEV, CS), BF16)


def _forward(place, tiles, own, other, kernels, alphas, routes, weights):
    frames = (TILE_FRAMES, TILE_DEV, CS)
    whole = pl.BlockSpec(memory_space=pltpu.VMEM)
    return pl.pallas_call(
        _forward_kernel,
        in_specs=[
            pl.BlockSpec(memory_space=pltpu.SMEM),
            whole,
        ]
        + [whole] * 15,
        out_specs=[whole] * 11,
        out_shape=[
            jax.ShapeDtypeStruct(frames, BF16),
            jax.ShapeDtypeStruct(frames, BF16),
            jax.ShapeDtypeStruct(frames, BF16),
            jax.ShapeDtypeStruct(frames, F32),
            jax.ShapeDtypeStruct(frames, F32),
            jax.ShapeDtypeStruct((LATENTS, CSO), BF16),
            jax.ShapeDtypeStruct((LATENTS, DL), F32),
            jax.ShapeDtypeStruct((CS // 128, CS, 128), BF16),
            jax.ShapeDtypeStruct((CSO // 128, KS * CS, 128), BF16),
            jax.ShapeDtypeStruct((DL // 128, CSO, 128), BF16),
            jax.ShapeDtypeStruct((8, WEIGHT_ROW + SHARE, CS), BF16),
        ],
        scratch_shapes=[
            pltpu.VMEM((CS // 128, DILATED_TAPS * CS, 128), BF16),
            pltpu.VMEM(frames, BF16),
        ],
        name="student_forward",
        compiler_params=pltpu.CompilerParams(vmem_limit_bytes=VMEM_LIMIT),
        cost_estimate=COST,
    )(place, tiles.reshape(ROWS, CS), *own, *other, *kernels, alphas, routes, weights)


def _stacked(values, columns):
    return jnp.concatenate(
        [values[:, start : start + columns] for start in range(0, values.shape[1], columns)], axis=0
    )


def _error_kernel(target_own, target_other, predicted, weights, proj, back_student, error):
    weight = weights[...] * (1.0 / LATENTS)
    for offset in range(OUTF):
        rows = slice(offset * TILE_DEV, (offset + 1) * TILE_DEV)
        target = target_own[rows, :] + target_other[rows, :].astype(F32)
        target = target.astype(BF16).astype(F32)
        error[rows, :] = (weight * (predicted[rows, :] - target)).astype(BF16)
    back = _dot_nt(error[...], _lanes(proj, slice(None))).astype(BF16)
    back_student[...] = back.reshape(OUTF, TILE_DEV, CSO)


def _error(targets, predicted, weights, proj):
    whole = pl.BlockSpec(memory_space=pltpu.VMEM)
    return pl.pallas_call(
        _error_kernel,
        in_specs=[whole] * 5,
        out_specs=[whole] * 2,
        out_shape=[
            jax.ShapeDtypeStruct((OUTF, TILE_DEV, CSO), BF16),
            jax.ShapeDtypeStruct((LATENTS, DL), BF16),
        ],
        name="error_backward",
        compiler_params=pltpu.CompilerParams(vmem_limit_bytes=VMEM_LIMIT),
        cost_estimate=COST,
    )(*targets, predicted, weights, proj)


def _down_kernel(place, parcels, rest_keep, rest_received, *refs):
    own, other, (keep, *sends), grads = refs[:4], refs[4:8], refs[8:12], refs[12]
    fsdp, chip = place[2], place[4]
    back = []
    for source in (own, other):
        for slab in range(SLABS):
            back += [_early(source, slab)[...], _late(source, slab)[...]]
    back = jnp.concatenate(back, axis=0)
    for tap in range(2):
        rows = []
        for side in range(2):
            for slab in range(SLABS):
                rows.append(parcels[chip ^ (2 * slab + side), tap * LATENTS : (tap + 1) * LATENTS, :])
        grads[tap * CS : (tap + 1) * CS, :] = _dot_tn(jnp.concatenate(rows, axis=0), back)
    for spot, out in enumerate((keep, *sends)):
        part = grads[pl.ds(pl.multiple_of((spot ^ fsdp) * 128, 128), 128), :]
        out[0:256, :] = _stacked(part, 256).astype(out.dtype)
        out[256:384, :] = (rest_keep[spot] + rest_received[spot].astype(F32)).astype(out.dtype)


def _down(place, parcels, rest, own, other):
    whole = pl.BlockSpec(memory_space=pltpu.VMEM)
    return pl.pallas_call(
        _down_kernel,
        in_specs=[pl.BlockSpec(memory_space=pltpu.SMEM)] + [whole] * 11,
        out_specs=[whole] * 4,
        out_shape=[jax.ShapeDtypeStruct((384, 256), F32)] + [jax.ShapeDtypeStruct((384, 256), BF16)] * 3,
        scratch_shapes=[pltpu.VMEM((CSO, CSO), F32)],
        name="down_gradient",
        compiler_params=pltpu.CompilerParams(vmem_limit_bytes=VMEM_LIMIT),
        cost_estimate=COST,
    )(place, parcels, *rest, *own, *other)


def _residual_kernel(
    place, back_student, error, student, down, mix, act_one, act_two, slope_two, slope_three,
    send, keep, back_three, back_residual, back_hidden, grad_dilated, grad_mix, grad_proj,
):
    me = place[1]
    back = back_student[...].reshape(LATENTS, CSO)
    for tap in range(KS):
        part = _dot_nt(back, _lanes(down, slice(tap * CS, (tap + 1) * CS)))
        for offset in range(OUTF):
            frame = STRIDE * offset - MARGIN + tap
            if 0 <= frame < TILE_FRAMES:
                piece = part[offset * TILE_DEV : (offset + 1) * TILE_DEV, :]
                if offset == 0 and frame >= MARGIN:
                    back_three[frame] += piece
                else:
                    back_three[frame] = piece
    for frame in range(0, TILE_FRAMES, 2):
        rows = slice(frame * TILE_DEV, (frame + 2) * TILE_DEV)
        shape = (2 * TILE_DEV, CS)
        share = back_three[frame : frame + 2].reshape(shape) * slope_three[frame : frame + 2].reshape(shape)
        share = share.astype(BF16)
        back_residual[rows, :] = share
        share = _dot_nt(share, _lanes(mix, slice(None))) * slope_two[frame : frame + 2].reshape(shape)
        back_hidden[rows, :] = share.astype(BF16)
    grad_mix[...] = _dot_tn(act_two[...].reshape(ROWS, CS), back_residual[...])
    half_taps = DILATED_TAPS // 2
    for tap in range(DILATED_TAPS):
        shift = UNIT_DILATION * (tap - half_taps)
        first, last = max(0, -shift), min(TILE_FRAMES, TILE_FRAMES - shift)
        rows = (last - first) * TILE_DEV
        grad_dilated[tap * CS : (tap + 1) * CS, :] = _dot_tn(
            act_one[first + shift : last + shift].reshape(rows, CS), back_hidden[first * TILE_DEV : last * TILE_DEV, :]
        )
    grad_proj[...] = _dot_tn(student[...], error[...])
    for place_index in range(CHUNKS):
        chunk = me ^ place_index
        part = jnp.concatenate(
            [
                _stacked(grad_proj[pl.ds(pl.multiple_of(chunk * 16, 16), 16), :], 256),
                grad_dilated[pl.ds(pl.multiple_of(chunk * 56, 8), 56), :],
                grad_mix[pl.ds(pl.multiple_of(chunk * 8, 8), 8), :],
            ],
            axis=0,
        )
        out = send if (place_index // 4) % 2 else keep
        out[(place_index // 8) * 4 + place_index % 4] = part.astype(out.dtype)


def _residual(place, back_student, error, student, down, mix, act_one, act_two, slope_two, slope_three):
    whole = pl.BlockSpec(memory_space=pltpu.VMEM)
    half = (CHUNKS // 2, 128, 256)
    return pl.pallas_call(
        _residual_kernel,
        in_specs=[pl.BlockSpec(memory_space=pltpu.SMEM)] + [whole] * 9,
        out_specs=[whole] * 2,
        out_shape=[jax.ShapeDtypeStruct(half, BF16), jax.ShapeDtypeStruct(half, F32)],
        scratch_shapes=[
            pltpu.VMEM((TILE_FRAMES, TILE_DEV, CS), F32),
            pltpu.VMEM((ROWS, CS), BF16),
            pltpu.VMEM((ROWS, CS), BF16),
            pltpu.VMEM((DILATED_TAPS * CS, CS), F32),
            pltpu.VMEM((CS, CS), F32),
            pltpu.VMEM((CSO, DL), F32),
        ],
        name="residual_backward",
        compiler_params=pltpu.CompilerParams(vmem_limit_bytes=VMEM_LIMIT),
        cost_estimate=COST,
    )(place, back_student, error, student, down, mix, act_one, act_two, slope_two, slope_three)


def _swap(values, axis, bit):
    return lax.ppermute(values, axis, [(i, i ^ bit) for i in range(lax.axis_size(axis))])


def on_device(
    student_tiles,
    teacher_tiles,
    send_list,
    clip_weight,
    kernel_dilated,
    kernel_mix,
    kernel_down,
    kernel_proj,
    kernel_teacher,
    alpha_one,
    alpha_two,
    alpha_three,
    alpha_teacher,
):
    n_dp = lax.axis_size("dp")
    d, f = lax.axis_index("dp"), lax.axis_index("fsdp")
    core, slab = d % 2, (d // 2) % SLABS
    halving = n_dp == 8
    me = d * N_FSDP + f if halving else jnp.int32(0)
    place = jnp.stack([core, me, f, slab, d % 8]).astype(jnp.int32)

    def plane_spread(early, late):
        return jnp.stack([early, _swap(early, "dp", 2)]), jnp.stack([late, _swap(late, "dp", 4)])

    def plane_gather(early, late):
        own = (early, _swap(early, "dp", 4), late, _swap(late, "dp", 2))
        return own, tuple(_swap(part, "dp", 1) for part in own)

    kernels = (kernel_dilated, kernel_mix, kernel_down, kernel_proj)
    flat_teacher = kernel_teacher.reshape(KS * QUARTER, DL)
    packed, columns = _pack(place, *kernels, flat_teacher)
    fetched = [_swap(packed, "fsdp", bit) for bit in range(1, N_FSDP)]
    columns = _swap(columns, "fsdp", 2)

    mine, sent = _teacher_act(place, teacher_tiles, alpha_teacher)
    fetched, sent = lax.optimization_barrier((fetched, sent))
    theirs = _swap(sent, "fsdp", 1)

    half = PACK_ROWS // 2
    spread = plane_spread(
        jnp.stack([part[:half] for part in fetched]), jnp.stack([part[half:] for part in fetched])
    )
    own, other = plane_gather(*spread)
    spread = plane_spread(columns[: KS * QUARTER // 2], columns[KS * QUARTER // 2 :])
    near = _teacher_near(mine, theirs, flat_teacher)
    teacher_own, teacher_other = plane_gather(*spread)
    own, other, _, near = lax.optimization_barrier((own, other, spread, near))

    alphas = jnp.stack([alpha_one, alpha_two, alpha_three])
    routes = send_list.reshape(-1)
    (
        act_one, act_two, act_three, slope_two, slope_three, student, predicted, mix, down, proj, parcel,
    ) = _forward(place, student_tiles, own, other, kernels, alphas, routes[:, None], clip_weight[:, None])
    near, predicted = lax.optimization_barrier((near, predicted))
    target, partial = _teacher_far(place, near, mine, theirs, teacher_own, teacher_other)
    targets = (target, _swap(partial, "fsdp", 1))

    latent_rows = parcel[:, WINDOW_ROWS:WEIGHT_ROW].reshape(8, OUTF * DL // CS, SHARE, CS)
    if halving:
        parcel, _ = lax.optimization_barrier((parcel, teacher_own))
        parcels = lax.all_to_all(parcel, "dp", split_axis=0, concat_axis=0, tiled=True)
        latent = parcels[:, WINDOW_ROWS:WEIGHT_ROW].reshape(8, OUTF * DL // CS, SHARE, CS).transpose(0, 2, 1, 3)
        slot_weights = jnp.sum(parcels[:, WEIGHT_ROW:, :3].astype(F32), axis=2).reshape(-1)
    else:
        latent = latent_rows.transpose(0, 2, 1, 3).reshape(TILE_DEV, OUTF * DL)
        latent = lax.all_to_all(latent, "dp", split_axis=0, concat_axis=0, tiled=True)
        slot_weights = lax.all_to_all(
            clip_weight.reshape(n_dp, TILE_DEV // n_dp), "dp", split_axis=0, concat_axis=0, tiled=True
        ).reshape(-1)
    latent = latent.reshape(TILE_DEV, OUTF, DL)
    hits = routes[:, None] == jnp.arange(TILE_DEV, dtype=jnp.int32)[None, :]
    weights = jnp.sum(jnp.where(hits, slot_weights[:, None], 0.0), axis=0)[:, None]

    back_student, error = _error(targets, predicted, weights, proj)
    send, keep = _residual(place, back_student, error, student, down, mix, act_one, act_two, slope_two, slope_three)

    if halving:
        keep = keep.reshape(2, 2, N_FSDP, 128, 256)
        received = _swap(send, "dp", 1).reshape(keep.shape)
        for bit in (4, 2):
            keep, out = keep[0] + received[0].astype(F32), (keep[1] + received[1].astype(F32)).astype(BF16)
            received = _swap(out, "dp", bit)
        part, *sends = _down(
            place, parcels, (keep, received), *plane_gather(*plane_spread(back_student[0], back_student[1]))
        )
        for bit, out in zip(range(1, N_FSDP), sends):
            part = part + _swap(out, "fsdp", bit).astype(F32)
        grad_down = jnp.concatenate([part[:128], part[128:256]], axis=1).reshape(-1)
        grad_proj = jnp.concatenate([part[256 + 16 * i : 272 + 16 * i] for i in range(4)], axis=1).reshape(-1)
        grad_dilated, grad_mix = part[320:376].reshape(-1), part[376:].reshape(-1)
    else:
        def joined(send, keep):
            rows = keep.shape[1]
            both = jnp.stack([keep.reshape(4, 4, rows, 256), send.astype(F32).reshape(4, 4, rows, 256)], axis=1)
            return both.reshape(CHUNKS, rows, 256)

        def scattered(values):
            return lax.psum_scatter(values.reshape(-1), ("dp", "fsdp"), scatter_dimension=0, tiled=True)

        part = joined(send, keep)
        windows = parcel[:, :WINDOW_ROWS].reshape(KS, OUTF, TILE_DEV, CS)
        grad_down = scattered(jnp.einsum("kotc,otd->kcd", windows, back_student, preferred_element_type=F32))
        grad_proj = scattered(jnp.concatenate([part[:, 16 * i : 16 * (i + 1)] for i in range(4)], axis=2))
        grad_dilated, grad_mix = scattered(part[:, 64:120]), scattered(part[:, 120:])
    return latent, grad_dilated, grad_mix, grad_down, grad_proj


def solution(mesh):
    placed = (
        P(("dp", "fsdp"), None, None),
        P(("dp", "fsdp"), None, None),
        P("dp", "fsdp", None),
        P(("dp", "fsdp")),
        P("fsdp", None),
        P("fsdp", None),
        P("fsdp", None),
        P("fsdp", None),
        P(None, "fsdp", None),
        P(),
        P(),
        P(),
        P(),
    )
    return jax.shard_map(
        on_device,
        mesh=mesh,
        in_specs=placed,
        out_specs=(
            P(("dp", "fsdp"), None, None),
            P(("dp", "fsdp")),
            P(("dp", "fsdp")),
            P(("dp", "fsdp")),
            P(("dp", "fsdp")),
        ),
        check_vma=False,
    )
```

```python
import jax
import jax.numpy as jnp
from jax import lax
from jax.experimental import pallas as pl
from jax.experimental.pallas import tpu as pltpu
from jax.sharding import PartitionSpec as P

CT = 512
DL = 1024
CS = 256
CSO = 512
KS = 16
STRIDE = 8
DILATED_TAPS = 7
UNIT_DILATION = 3
TILE_FRAMES = 16
TILE_DEV = 128
CHUNKS = 32
OUTF = 2
MARGIN = (KS - STRIDE) // 2
SHARE = TILE_DEV // 8
WINDOW_ROWS = 2 * OUTF * TILE_DEV
PARCEL_ROWS = WINDOW_ROWS + OUTF * DL // CS * SHARE
ROWS = TILE_DEV * TILE_FRAMES
LATENTS = TILE_DEV * OUTF
N_FSDP = 4
QUARTER = CT // N_FSDP
GROUP = 16
SLABS = 4
F32 = jnp.float32
BF16 = jnp.bfloat16
VMEM_LIMIT = 48 * 1024 * 1024
COST = pl.CostEstimate(flops=1000, bytes_accessed=1000, transcendentals=0)

PACK = {
    "dilated": DILATED_TAPS * CS // N_FSDP // SLABS,
    "mix": CS // N_FSDP // SLABS,
    "down": KS * CS // N_FSDP // SLABS,
    "proj": CSO // N_FSDP // SLABS,
}
PACK_COLS = {"dilated": 1, "mix": 1, "down": 2, "proj": 4}
PACK_ROWS = sum(PACK[name] * PACK_COLS[name] for name in PACK)

INV_PI = 0.3183098861837907
PI_PARTS = (3.125, 0.015625, 9.67502593994140625e-4, 1.509957990978376432e-7)
SIN_TERMS = (0.9999999765137553, -0.16666647593489264, 0.008332899222829617, -0.0001980086530702378, 2.5904300303557895e-06)
COS_TERMS = (0.999999953036273, -0.4999990494860951, 0.0416635772644784, -0.0013853657929132671, 2.3153011971441464e-05)


def _reduced(angle):
    turns = jnp.round(angle * INV_PI)
    for part in PI_PARTS:
        angle = angle - turns * part
    return angle


def _series(square, terms):
    total = square * terms[-1] + terms[-2]
    for term in terms[-3::-1]:
        total = total * square + term
    return total


def _snake(values, alpha, inverse):
    angle = _reduced(alpha * values)
    sine = angle * _series(angle * angle, SIN_TERMS)
    return values + sine * sine * inverse


def _snake_and_slope(values, alpha, inverse):
    angle = _reduced(alpha * values)
    square = angle * angle
    sine = angle * _series(square, SIN_TERMS)
    cosine = _series(square, COS_TERMS)
    return values + sine * sine * inverse, 1.0 + 2.0 * sine * cosine


def _dot(left, right):
    return jnp.dot(left, right, preferred_element_type=F32)


def _dot_nt(left, right):
    return lax.dot_general(left, right, (((1,), (1,)), ((), ())), preferred_element_type=F32)


def _dot_tn(left, right):
    return lax.dot_general(left, right, (((0,), (0,)), ((), ())), preferred_element_type=F32)


def _turn():
    count = GROUP * TILE_FRAMES
    target = lax.broadcasted_iota(jnp.int32, (count, count), 0)
    source = lax.broadcasted_iota(jnp.int32, (count, count), 1)
    wanted = (target % GROUP) * TILE_FRAMES + target // GROUP
    return jnp.where(source == wanted, 1.0, 0.0).astype(BF16)


def _teacher_act_kernel(place, tiles, alpha, keep, send):
    fsdp = place[2]
    turn = _turn()
    for out, first in ((keep, fsdp), (send, fsdp ^ 1)):
        for index in range(2):
            lanes = pl.ds(pl.multiple_of((first ^ (2 * index)) * QUARTER, QUARTER), QUARTER)
            scale = alpha[:, lanes]
            acted = _snake(_dot(turn, tiles[:, lanes]), scale, 1.0 / scale).astype(BF16)
            out[index] = acted.reshape(TILE_FRAMES, GROUP, QUARTER)


def _teacher_act(place, tiles, alpha):
    steps = TILE_DEV // GROUP
    shape = jax.ShapeDtypeStruct((2, TILE_FRAMES, TILE_DEV, QUARTER), BF16)
    return pl.pallas_call(
        _teacher_act_kernel,
        grid=(steps,),
        in_specs=[
            pl.BlockSpec(memory_space=pltpu.SMEM),
            pl.BlockSpec((GROUP * TILE_FRAMES, CT), lambda i: (i, 0)),
            pl.BlockSpec((1, CT), lambda i: (0, 0)),
        ],
        out_specs=[pl.BlockSpec((2, TILE_FRAMES, GROUP, QUARTER), lambda i: (0, 0, i, 0))] * 2,
        out_shape=[shape] * 2,
        name="teacher_act",
        compiler_params=pltpu.CompilerParams(vmem_limit_bytes=VMEM_LIMIT),
        cost_estimate=COST,
    )(place, tiles.reshape(ROWS, CT), alpha.reshape(1, CT))


def _pack_kernel(place, dilated, mix, down, proj, teacher, packed, early, late, sems):
    core, slab = place[0], place[3]
    copies = []
    row = 0
    for name, source in (("dilated", dilated), ("mix", mix), ("down", down), ("proj", proj)):
        rows = PACK[name]
        for block in range(PACK_COLS[name]):
            begin = pl.multiple_of((core * PACK_COLS[name] + block) * 128, 128)
            copies.append(pltpu.make_async_copy(
                source.at[pl.ds(pl.multiple_of(slab * rows, 16), rows), pl.ds(begin, 128)],
                packed.at[pl.ds(row, rows), :],
                sems.at[len(copies)],
            ))
            row += rows
    begin = pl.multiple_of((core * SLABS + slab) * 128, 128)
    half = KS * QUARTER // 2
    for index, out in enumerate((early, late)):
        source = teacher.at[index * half : (index + 1) * half, pl.ds(begin, 128)]
        copies.append(pltpu.make_async_copy(source, out, sems.at[len(copies)]))
    for copy in copies:
        copy.start()
    for copy in copies:
        copy.wait()


def _pack(place, *kernels):
    anywhere = pl.BlockSpec(memory_space=pl.ANY)
    return pl.pallas_call(
        _pack_kernel,
        in_specs=[pl.BlockSpec(memory_space=pltpu.SMEM)] + [anywhere] * 5,
        out_specs=[pl.BlockSpec(memory_space=pltpu.VMEM)] * 3,
        out_shape=[
            jax.ShapeDtypeStruct((PACK_ROWS, 128), BF16),
            jax.ShapeDtypeStruct((KS * QUARTER // 2, 128), BF16),
            jax.ShapeDtypeStruct((KS * QUARTER // 2, 128), BF16),
        ],
        scratch_shapes=[pltpu.SemaphoreType.DMA((10,))],
        name="pack_kernels",
        cost_estimate=COST,
    )(place, *kernels)


def _early(parts, slab):
    return parts[slab // 2].at[slab % 2]


def _late(parts, slab):
    return parts[2 + slab % 2].at[slab // 2]


def _windows(mine, theirs, quarter, offset):
    first = max(0, STRIDE * offset - MARGIN)
    wide = [
        jnp.concatenate([tiles[quarter, first + step] for step in range(STRIDE + MARGIN)], axis=1)
        for tiles in (mine, theirs)
    ]
    return jnp.concatenate(wide, axis=0), first - (STRIDE * offset - MARGIN)


def _teacher_near_kernel(mine, theirs, kernel, out):
    for offset in range(OUTF):
        wide, tap = _windows(mine, theirs, 0, offset)
        part = _dot(wide, kernel[tap * QUARTER : (tap + STRIDE + MARGIN) * QUARTER, :])
        for device in range(2):
            start = device * LATENTS + offset * TILE_DEV
            out[start : start + TILE_DEV, :] = part[device * TILE_DEV : (device + 1) * TILE_DEV, :]


def _teacher_near(mine, theirs, kernel):
    return pl.pallas_call(
        _teacher_near_kernel,
        out_shape=jax.ShapeDtypeStruct((2 * LATENTS, DL), F32),
        name="teacher_near",
        compiler_params=pltpu.CompilerParams(vmem_limit_bytes=VMEM_LIMIT),
        cost_estimate=COST,
    )(mine, theirs, kernel)


def _teacher_far_kernel(place, near, mine, theirs, *refs):
    own, other, (keep, send) = refs[:4], refs[4:8], refs[8:]
    core, plane = place[0], place[3]
    taps = KS // 2 * QUARTER
    skipped = MARGIN * QUARTER
    for offset in range(OUTF):
        wide, tap = _windows(mine, theirs, 1, offset)
        for side, source in enumerate((own, other)):
            for pair in range(0, SLABS, 2):
                columns = []
                for slab in (pair, pair + 1):
                    early, late = _early(source, slab)[...], _late(source, slab)[...]
                    if tap:
                        columns.append(jnp.concatenate([early[skipped:], late], axis=0))
                    else:
                        columns.append(jnp.concatenate([early, late[: taps - skipped]], axis=0))
                part = _dot(wide, jnp.concatenate(columns, axis=1))
                for index, slab in enumerate((pair, pair + 1)):
                    block = (core ^ side) * SLABS + (plane ^ slab)
                    lanes = pl.ds(pl.multiple_of(block * 128, 128), 128)
                    for device, out in enumerate((keep, send)):
                        piece = part[device * TILE_DEV : (device + 1) * TILE_DEV, index * 128 : (index + 1) * 128]
                        start = device * LATENTS + offset * TILE_DEV
                        piece += near[start : start + TILE_DEV, lanes]
                        out[offset * TILE_DEV : (offset + 1) * TILE_DEV, lanes] = piece.astype(out.dtype)


def _teacher_far(place, near, mine, theirs, own, other):
    whole = pl.BlockSpec(memory_space=pltpu.VMEM)
    return pl.pallas_call(
        _teacher_far_kernel,
        in_specs=[pl.BlockSpec(memory_space=pltpu.SMEM)] + [whole] * 11,
        out_specs=[whole] * 2,
        out_shape=[jax.ShapeDtypeStruct((LATENTS, DL), F32), jax.ShapeDtypeStruct((LATENTS, DL), BF16)],
        name="teacher_far",
        compiler_params=pltpu.CompilerParams(vmem_limit_bytes=VMEM_LIMIT),
        cost_estimate=COST,
    )(place, near, mine, theirs, *own, *other)


def _lanes(blocks, rows):
    return jnp.concatenate([blocks[index, rows, :] for index in range(blocks.shape[0])], axis=1)


def _forward_kernel(
    place, tiles, own_a, own_b, own_c, own_d, other_a, other_b, other_c, other_d,
    near_dilated, near_mix, near_down, near_proj, alphas, routes,
    act_one, act_two, act_three, slope_two, slope_three, student, predicted, mix, down, proj, parcel,
    dilated, held,
):
    own, other = (own_a, own_b, own_c, own_d), (other_a, other_b, other_c, other_d)
    core, fsdp, plane = place[0], place[2], place[3]

    def rows_of(quarter, slab, share):
        return pl.ds(pl.multiple_of(quarter * (SLABS * share) + slab * share, 16), share)

    kinds = ((near_dilated, dilated), (near_mix, mix), (near_down, down), (near_proj, proj))
    for name, (source, target) in zip(PACK, kinds):
        rows = pl.ds(pl.multiple_of(fsdp * (SLABS * PACK[name]), 16), SLABS * PACK[name])
        for block in range(target.shape[0]):
            target[block, rows, :] = source[:, block * 128 : (block + 1) * 128]
    for flip, pieces in enumerate((own, other)):
        side = core ^ flip
        for slab in range(SLABS):
            for bit in range(1, N_FSDP):
                early, late = _early(pieces, slab).at[bit - 1], _late(pieces, slab).at[bit - 1]
                quarter, chip = fsdp ^ bit, plane ^ slab
                dilated[side, rows_of(quarter, chip, PACK["dilated"]), :] = early[0:112, :]
                mix[side, rows_of(quarter, chip, PACK["mix"]), :] = early[112:128, :]
                rows = rows_of(quarter, chip, PACK["down"])
                down[side * 2, rows, :] = early[128:384, :]
                down[side * 2 + 1, rows, :] = late[0:256, :]
                rows = rows_of(quarter, chip, PACK["proj"])
                for block in range(4):
                    proj[side * 4 + block, rows, :] = late[256 + block * 32 : 288 + block * 32, :]

    alpha_one, alpha_two, alpha_three = alphas[0:1, :], alphas[1:2, :], alphas[2:3, :]
    inverse_one, inverse_two, inverse_three = 1.0 / alpha_one, 1.0 / alpha_two, 1.0 / alpha_three
    turn = _turn()
    for step in range(TILE_DEV // GROUP):
        turned = _dot(turn, tiles[step * GROUP * TILE_FRAMES : (step + 1) * GROUP * TILE_FRAMES, :])
        shape = (TILE_FRAMES, GROUP, CS)
        held[:, step * GROUP : (step + 1) * GROUP, :] = turned.astype(BF16).reshape(shape)
        acted = _snake(turned, alpha_one, inverse_one).astype(BF16)
        act_one[:, step * GROUP : (step + 1) * GROUP, :] = acted.reshape(shape)

    half_taps = DILATED_TAPS // 2
    spans = []
    for frame in range(TILE_FRAMES):
        valid = [tap for tap in range(DILATED_TAPS) if 0 <= frame + UNIT_DILATION * (tap - half_taps) < TILE_FRAMES]
        span = (valid[0], valid[-1] + 1)
        if spans and spans[-1][2] == span:
            spans[-1][1] = frame + 1
        else:
            spans.append([frame, frame + 1, span])
    for start, stop, (low, high) in spans:
        wide = jnp.concatenate(
            [
                act_one[start + shift : stop + shift].reshape((stop - start) * TILE_DEV, CS)
                for shift in (UNIT_DILATION * (tap - half_taps) for tap in range(low, high))
            ],
            axis=1,
        )
        hidden = _dot(wide, _lanes(dilated, slice(low * CS, high * CS)))
        acted, slope = _snake_and_slope(hidden, alpha_two, inverse_two)
        shape = (stop - start, TILE_DEV, CS)
        acted = acted.astype(BF16)
        act_two[start:stop] = acted.reshape(shape)
        slope_two[start:stop] = slope.reshape(shape)
        residual = held[start:stop].reshape((stop - start) * TILE_DEV, CS).astype(F32) + _dot(acted, _lanes(mix, slice(None)))
        acted, slope = _snake_and_slope(residual, alpha_three, inverse_three)
        act_three[start:stop] = acted.astype(BF16).reshape(shape)
        slope_three[start:stop] = slope.reshape(shape)

    reach = STRIDE + MARGIN
    for offset in range(OUTF):
        first = max(0, STRIDE * offset - MARGIN)
        tap = first - (STRIDE * offset - MARGIN)
        wide = jnp.concatenate([act_three[first + step] for step in range(reach)], axis=1)
        part = _dot(wide, _lanes(down, slice(tap * CS, (tap + reach) * CS)))
        student[offset * TILE_DEV : (offset + 1) * TILE_DEV, :] = part.astype(BF16)
    pick = jnp.where(
        routes[...] == lax.broadcasted_iota(jnp.int32, (TILE_DEV, TILE_DEV), 1), 1.0, 0.0
    ).astype(BF16)
    for offset in range(OUTF):
        rows = slice(offset * TILE_DEV, (offset + 1) * TILE_DEV)
        part = _dot(student[rows, :], _lanes(proj, slice(None)))
        predicted[rows, :] = part
        picked = _dot(pick, part.astype(BF16)).astype(BF16)
        for block in range(DL // CS):
            row = WINDOW_ROWS + (offset * (DL // CS) + block) * SHARE
            for owner in range(8):
                parcel[owner, row : row + SHARE, :] = picked[
                    owner * SHARE : (owner + 1) * SHARE, block * CS : (block + 1) * CS
                ]
    for tap in range(KS):
        for offset in range(OUTF):
            frame = STRIDE * offset - MARGIN + tap
            row = (tap % 2 * OUTF + offset) * TILE_DEV
            if 0 <= frame < TILE_FRAMES:
                parcel[tap // 2, row : row + TILE_DEV, :] = act_three[frame]
            else:
                parcel[tap // 2, row : row + TILE_DEV, :] = jnp.zeros((TILE_DEV, CS), BF16)


def _forward(place, tiles, own, other, kernels, alphas, routes):
    frames = (TILE_FRAMES, TILE_DEV, CS)
    whole = pl.BlockSpec(memory_space=pltpu.VMEM)
    return pl.pallas_call(
        _forward_kernel,
        in_specs=[
            pl.BlockSpec(memory_space=pltpu.SMEM),
            whole,
        ]
        + [whole] * 14,
        out_specs=[whole] * 11,
        out_shape=[
            jax.ShapeDtypeStruct(frames, BF16),
            jax.ShapeDtypeStruct(frames, BF16),
            jax.ShapeDtypeStruct(frames, BF16),
            jax.ShapeDtypeStruct(frames, F32),
            jax.ShapeDtypeStruct(frames, F32),
            jax.ShapeDtypeStruct((LATENTS, CSO), BF16),
            jax.ShapeDtypeStruct((LATENTS, DL), F32),
            jax.ShapeDtypeStruct((CS // 128, CS, 128), BF16),
            jax.ShapeDtypeStruct((CSO // 128, KS * CS, 128), BF16),
            jax.ShapeDtypeStruct((DL // 128, CSO, 128), BF16),
            jax.ShapeDtypeStruct((8, PARCEL_ROWS, CS), BF16),
        ],
        scratch_shapes=[
            pltpu.VMEM((CS // 128, DILATED_TAPS * CS, 128), BF16),
            pltpu.VMEM(frames, BF16),
        ],
        name="student_forward",
        compiler_params=pltpu.CompilerParams(vmem_limit_bytes=VMEM_LIMIT),
        cost_estimate=COST,
    )(place, tiles.reshape(ROWS, CS), *own, *other, *kernels, alphas, routes)


def _stacked(values, columns):
    return jnp.concatenate(
        [values[:, start : start + columns] for start in range(0, values.shape[1], columns)], axis=0
    )


def _error_kernel(
    place, target_own, target_other, predicted, weights, student, proj, back_student, send, keep, error, grad_proj
):
    me = place[1]
    weight = weights[...] * (1.0 / LATENTS)
    for offset in range(OUTF):
        rows = slice(offset * TILE_DEV, (offset + 1) * TILE_DEV)
        target = target_own[rows, :] + target_other[rows, :].astype(F32)
        target = target.astype(BF16).astype(F32)
        error[rows, :] = (weight * (predicted[rows, :] - target)).astype(BF16)
    back = _dot_nt(error[...], _lanes(proj, slice(None))).astype(BF16)
    back_student[...] = back.reshape(OUTF, TILE_DEV, CSO)
    grad_proj[...] = _dot_tn(student[...], error[...])
    for spot in range(CHUNKS):
        share = grad_proj[pl.ds(pl.multiple_of((me ^ spot) * 16, 16), 16), :]
        out = send if (spot // 4) % 2 else keep
        out[(spot // 8 % 2) * 8 + (spot // 16) * 4 + spot % 4] = _stacked(share, 256).astype(out.dtype)


def _error(place, targets, predicted, weights, student, proj):
    half = (CHUNKS // 2, 64, 256)
    whole = pl.BlockSpec(memory_space=pltpu.VMEM)
    return pl.pallas_call(
        _error_kernel,
        in_specs=[pl.BlockSpec(memory_space=pltpu.SMEM)] + [whole] * 6,
        out_specs=[whole] * 3,
        out_shape=[
            jax.ShapeDtypeStruct((OUTF, TILE_DEV, CSO), BF16),
            jax.ShapeDtypeStruct(half, BF16),
            jax.ShapeDtypeStruct(half, F32),
        ],
        scratch_shapes=[pltpu.VMEM((LATENTS, DL), BF16), pltpu.VMEM((CSO, DL), F32)],
        name="error_backward",
        compiler_params=pltpu.CompilerParams(vmem_limit_bytes=60 * 1024 * 1024),
        cost_estimate=COST,
    )(place, *targets, predicted, weights, student, proj)


def _down_kernel(place, parcels, *refs):
    own, other, (keep, *sends), grads = refs[:4], refs[4:8], refs[8:12], refs[12]
    fsdp, chip = place[2], place[4]
    back = []
    for source in (own, other):
        for slab in range(SLABS):
            back += [_early(source, slab)[...], _late(source, slab)[...]]
    back = jnp.concatenate(back, axis=0)
    for tap in range(2):
        rows = []
        for side in range(2):
            for slab in range(SLABS):
                rows.append(parcels[chip ^ (2 * slab + side), tap * LATENTS : (tap + 1) * LATENTS, :])
        grads[tap * CS : (tap + 1) * CS, :] = _dot_tn(jnp.concatenate(rows, axis=0), back)
    for spot, out in enumerate((keep, *sends)):
        part = grads[pl.ds(pl.multiple_of((spot ^ fsdp) * 128, 128), 128), :]
        out[...] = part.astype(out.dtype)


def _down(place, parcels, own, other):
    whole = pl.BlockSpec(memory_space=pltpu.VMEM)
    return pl.pallas_call(
        _down_kernel,
        in_specs=[pl.BlockSpec(memory_space=pltpu.SMEM)] + [whole] * 9,
        out_specs=[whole] * 4,
        out_shape=[jax.ShapeDtypeStruct((128, CSO), F32)] + [jax.ShapeDtypeStruct((128, CSO), BF16)] * 3,
        scratch_shapes=[pltpu.VMEM((CSO, CSO), F32)],
        name="down_gradient",
        compiler_params=pltpu.CompilerParams(vmem_limit_bytes=VMEM_LIMIT),
        cost_estimate=COST,
    )(place, parcels, *own, *other)


def _flat(out, values):
    blocks = values.shape[1] // 128
    for block in range(blocks):
        out[pl.ds(block, values.shape[0], stride=blocks), :] = values[:, block * 128 : (block + 1) * 128]


def _finish_kernel(down, rest_proj, rest_other, *refs):
    downs, rests, (dilated, mix, full_down, proj) = refs[:3], refs[3:6], refs[6:]
    total = down[...]
    for part in downs:
        total += part[...].astype(F32)
    _flat(full_down, total)
    total = jnp.concatenate([rest_proj[...], rest_other[...]], axis=0)
    for part in rests:
        total += part[...].astype(F32)
    _flat(proj, jnp.concatenate([total[16 * i : 16 * (i + 1)] for i in range(4)], axis=1))
    _flat(dilated, total[64:120])
    _flat(mix, total[120:128])


def _finish(down, downs, rest, rests):
    whole = pl.BlockSpec(memory_space=pltpu.VMEM)
    return pl.pallas_call(
        _finish_kernel,
        in_specs=[whole] * 9,
        out_specs=[whole] * 4,
        out_shape=[jax.ShapeDtypeStruct((rows, 128), F32) for rows in (112, 16, 512, 128)],
        name="finish_gradients",
        compiler_params=pltpu.CompilerParams(vmem_limit_bytes=VMEM_LIMIT),
        cost_estimate=COST,
    )(down, *rest, *downs, *rests)


def _residual_kernel(
    place, back_student, down, mix, act_one, act_two, slope_two, slope_three,
    send, keep, back_three, back_residual, back_hidden, grad_dilated, grad_mix,
):
    me = place[1]
    back = back_student[...].reshape(LATENTS, CSO)
    for tap in range(KS):
        part = _dot_nt(back, _lanes(down, slice(tap * CS, (tap + 1) * CS)))
        for offset in range(OUTF):
            frame = STRIDE * offset - MARGIN + tap
            if 0 <= frame < TILE_FRAMES:
                piece = part[offset * TILE_DEV : (offset + 1) * TILE_DEV, :]
                if offset == 0 and frame >= MARGIN:
                    back_three[frame] += piece
                else:
                    back_three[frame] = piece
    for frame in range(0, TILE_FRAMES, 2):
        rows = slice(frame * TILE_DEV, (frame + 2) * TILE_DEV)
        shape = (2 * TILE_DEV, CS)
        share = back_three[frame : frame + 2].reshape(shape) * slope_three[frame : frame + 2].reshape(shape)
        share = share.astype(BF16)
        back_residual[rows, :] = share
        share = _dot_nt(share, _lanes(mix, slice(None))) * slope_two[frame : frame + 2].reshape(shape)
        back_hidden[rows, :] = share.astype(BF16)
    grad_mix[...] = _dot_tn(act_two[...].reshape(ROWS, CS), back_residual[...])
    half_taps = DILATED_TAPS // 2
    for tap in range(DILATED_TAPS):
        shift = UNIT_DILATION * (tap - half_taps)
        first, last = max(0, -shift), min(TILE_FRAMES, TILE_FRAMES - shift)
        rows = (last - first) * TILE_DEV
        grad_dilated[tap * CS : (tap + 1) * CS, :] = _dot_tn(
            act_one[first + shift : last + shift].reshape(rows, CS), back_hidden[first * TILE_DEV : last * TILE_DEV, :]
        )
    for place_index in range(CHUNKS):
        chunk = me ^ place_index
        part = jnp.concatenate(
            [
                grad_dilated[pl.ds(pl.multiple_of(chunk * 56, 8), 56), :],
                grad_mix[pl.ds(pl.multiple_of(chunk * 8, 8), 8), :],
            ],
            axis=0,
        )
        out = send if (place_index // 4) % 2 else keep
        out[(place_index // 8) * 4 + place_index % 4] = part.astype(out.dtype)


def _residual(place, back_student, down, mix, act_one, act_two, slope_two, slope_three):
    whole = pl.BlockSpec(memory_space=pltpu.VMEM)
    half = (CHUNKS // 2, 64, 256)
    return pl.pallas_call(
        _residual_kernel,
        in_specs=[pl.BlockSpec(memory_space=pltpu.SMEM)] + [whole] * 7,
        out_specs=[whole] * 2,
        out_shape=[jax.ShapeDtypeStruct(half, BF16), jax.ShapeDtypeStruct(half, F32)],
        scratch_shapes=[
            pltpu.VMEM((TILE_FRAMES, TILE_DEV, CS), F32),
            pltpu.VMEM((ROWS, CS), BF16),
            pltpu.VMEM((ROWS, CS), BF16),
            pltpu.VMEM((DILATED_TAPS * CS, CS), F32),
            pltpu.VMEM((CS, CS), F32),
        ],
        name="residual_backward",
        compiler_params=pltpu.CompilerParams(vmem_limit_bytes=VMEM_LIMIT),
        cost_estimate=COST,
    )(place, back_student, down, mix, act_one, act_two, slope_two, slope_three)


def _swap(values, axis, bit):
    return lax.ppermute(values, axis, [(i, i ^ bit) for i in range(lax.axis_size(axis))])


def on_device(
    student_tiles,
    teacher_tiles,
    send_list,
    clip_weight,
    kernel_dilated,
    kernel_mix,
    kernel_down,
    kernel_proj,
    kernel_teacher,
    alpha_one,
    alpha_two,
    alpha_three,
    alpha_teacher,
):
    n_dp = lax.axis_size("dp")
    d, f = lax.axis_index("dp"), lax.axis_index("fsdp")
    core, slab = d % 2, (d // 2) % SLABS
    halving = n_dp == 8
    me = d * N_FSDP + f if halving else jnp.int32(0)
    place = jnp.stack([core, me, f, slab, d % 8]).astype(jnp.int32)

    def plane_spread(early, late):
        return jnp.stack([early, _swap(early, "dp", 2)]), jnp.stack([late, _swap(late, "dp", 4)])

    def plane_gather(early, late):
        return early, _swap(early, "dp", 4), late, _swap(late, "dp", 2)

    def core_gather(own):
        return own, tuple(_swap(part, "dp", 1) for part in own)

    kernels = (kernel_dilated, kernel_mix, kernel_down, kernel_proj)
    flat_teacher = kernel_teacher.reshape(KS * QUARTER, DL)
    packed, early, late = _pack(place, *kernels, flat_teacher)
    fetched = [_swap(packed, "fsdp", bit) for bit in range(1, N_FSDP)]
    early, late = _swap(early, "fsdp", 2), _swap(late, "fsdp", 2)

    routes = send_list.reshape(-1)
    slot_weights = lax.all_to_all(
        clip_weight.reshape(n_dp, TILE_DEV // n_dp), "dp", split_axis=0, concat_axis=0, tiled=True
    ).reshape(-1)
    hits = routes[:, None] == jnp.arange(TILE_DEV, dtype=jnp.int32)[None, :]
    weights = jnp.sum(jnp.where(hits, slot_weights[:, None], 0.0), axis=0)[:, None]

    mine, sent = _teacher_act(place, teacher_tiles, alpha_teacher)
    fetched, sent, weights = lax.optimization_barrier((fetched, sent, weights))
    theirs = _swap(sent, "fsdp", 1)

    half = PACK_ROWS // 2
    spread = plane_spread(
        jnp.stack([part[:half] for part in fetched]), jnp.stack([part[half:] for part in fetched])
    )
    spread, early = lax.optimization_barrier((spread, early))
    own, other = core_gather(plane_gather(*spread))
    early, late, _ = lax.optimization_barrier((early, late, own))
    spread = plane_spread(early, late)
    teacher_own = plane_gather(*spread)
    own, other, _ = lax.optimization_barrier((own, other, spread))

    alphas = jnp.stack([alpha_one, alpha_two, alpha_three])
    (
        act_one, act_two, act_three, slope_two, slope_three, student, predicted, mix, down, proj, parcel,
    ) = _forward(place, student_tiles, own, other, kernels, alphas, routes[:, None])
    theirs, teacher_own, predicted = lax.optimization_barrier((theirs, teacher_own, predicted))
    teacher_own, teacher_other = core_gather(teacher_own)
    near = _teacher_near(mine, theirs, flat_teacher)
    target, partial = _teacher_far(place, near, mine, theirs, teacher_own, teacher_other)
    targets = (target, _swap(partial, "fsdp", 1))

    latent_rows = parcel[:, WINDOW_ROWS:].reshape(8, OUTF * DL // CS, SHARE, CS)
    if halving:
        parcels = lax.all_to_all(parcel, "dp", split_axis=0, concat_axis=0, tiled=True)
        latent = parcels[:, WINDOW_ROWS:].reshape(8, OUTF * DL // CS, SHARE, CS).transpose(0, 2, 1, 3)
    else:
        latent = latent_rows.transpose(0, 2, 1, 3).reshape(TILE_DEV, OUTF * DL)
        latent = lax.all_to_all(latent, "dp", split_axis=0, concat_axis=0, tiled=True)
    latent = latent.reshape(TILE_DEV, OUTF, DL)
    back_student, send_a, keep_a = _error(place, targets, predicted, weights, student, proj)
    send_b, keep_b = _residual(place, back_student, down, mix, act_one, act_two, slope_two, slope_three)

    if halving:
        def reduce_plane(send, keep, order):
            keep = keep.reshape(2, 2, N_FSDP, 64, 256)
            received = _swap(send, "dp", 1).reshape(keep.shape)
            for bit in (2, 4) if order == "xy" else (4, 2):
                keep, out = keep[0] + received[0].astype(F32), (keep[1] + received[1].astype(F32)).astype(BF16)
                received = _swap(out, "dp", bit)
            return keep + received.astype(F32)

        back_student, parcels = lax.optimization_barrier((back_student, parcels))
        keep_d, *sends = _down(place, parcels, *core_gather(plane_gather(*plane_spread(back_student[0], back_student[1]))))
        downs = [_swap(out, "fsdp", bit) for bit, out in zip(range(1, N_FSDP), sends)]
        rest_a, rest_b = reduce_plane(send_a, keep_a, "xy"), reduce_plane(send_b, keep_b, "yx")
        rest = jnp.concatenate([rest_a, rest_b], axis=1)
        rests = [_swap(rest[bit].astype(BF16), "fsdp", bit) for bit in range(1, N_FSDP)]
        grads = _finish(keep_d, downs, (rest_a[0], rest_b[0]), rests)
        grad_dilated, grad_mix, grad_down, grad_proj = [grad.reshape(-1) for grad in grads]
    else:
        def joined(send, keep):
            rows = keep.shape[-2]
            both = jnp.stack([keep.reshape(4, 4, rows, 256), send.astype(F32).reshape(4, 4, rows, 256)], axis=1)
            return both.reshape(CHUNKS, rows, 256)

        def scattered(values):
            return lax.psum_scatter(values.reshape(-1), ("dp", "fsdp"), scatter_dimension=0, tiled=True)

        turned = [jnp.swapaxes(half.reshape(2, 2, N_FSDP, 64, 256), 0, 1) for half in (send_a, keep_a)]
        part = jnp.concatenate([joined(*turned), joined(send_b, keep_b)], axis=1)
        windows = parcel[:, :WINDOW_ROWS].reshape(KS, OUTF, TILE_DEV, CS)
        grad_down = scattered(jnp.einsum("kotc,otd->kcd", windows, back_student, preferred_element_type=F32))
        grad_proj = scattered(jnp.concatenate([part[:, 16 * i : 16 * (i + 1)] for i in range(4)], axis=2))
        grad_dilated, grad_mix = scattered(part[:, 64:120]), scattered(part[:, 120:])
    return latent, grad_dilated, grad_mix, grad_down, grad_proj


def solution(mesh):
    placed = (
        P(("dp", "fsdp"), None, None),
        P(("dp", "fsdp"), None, None),
        P("dp", "fsdp", None),
        P(("dp", "fsdp")),
        P("fsdp", None),
        P("fsdp", None),
        P("fsdp", None),
        P("fsdp", None),
        P(None, "fsdp", None),
        P(),
        P(),
        P(),
        P(),
    )
    return jax.shard_map(
        on_device,
        mesh=mesh,
        in_specs=placed,
        out_specs=(
            P(("dp", "fsdp"), None, None),
            P(("dp", "fsdp")),
            P(("dp", "fsdp")),
            P(("dp", "fsdp")),
            P(("dp", "fsdp")),
        ),
        check_vma=False,
    )
```

```python
import jax
import jax.numpy as jnp
from jax import lax
from jax.experimental import pallas as pl
from jax.experimental.pallas import tpu as pltpu
from jax.sharding import PartitionSpec as P

CT = 512
DL = 1024
CS = 256
CSO = 512
KS = 16
STRIDE = 8
DILATED_TAPS = 7
UNIT_DILATION = 3
TILE_FRAMES = 16
TILE_DEV = 128
CHUNKS = 32
OUTF = 2
MARGIN = (KS - STRIDE) // 2
SHARE = TILE_DEV // 8
WINDOW_ROWS = 2 * OUTF * TILE_DEV
PARCEL_ROWS = WINDOW_ROWS + OUTF * DL // CS * SHARE
ROWS = TILE_DEV * TILE_FRAMES
LATENTS = TILE_DEV * OUTF
N_FSDP = 4
QUARTER = CT // N_FSDP
GROUP = 16
SLABS = 4
F32 = jnp.float32
BF16 = jnp.bfloat16
VMEM_LIMIT = 48 * 1024 * 1024
WHOLE_VMEM = 60 * 1024 * 1024
COST = pl.CostEstimate(flops=1000, bytes_accessed=1000, transcendentals=0)

PACK = {
    "dilated": DILATED_TAPS * CS // N_FSDP // SLABS,
    "mix": CS // N_FSDP // SLABS,
    "down": KS * CS // N_FSDP // SLABS,
    "proj": CSO // N_FSDP // SLABS,
}
PACK_COLS = {"dilated": 1, "mix": 1, "down": 2, "proj": 4}
PACK_ROWS = sum(PACK[name] * PACK_COLS[name] for name in PACK)

INV_PI = 0.3183098861837907
PI_PARTS = (3.125, 0.015625, 9.67502593994140625e-4, 1.509957990978376432e-7)
SIN_TERMS = (0.9999999765137553, -0.16666647593489264, 0.008332899222829617, -0.0001980086530702378, 2.5904300303557895e-06)
COS_TERMS = (0.999999953036273, -0.4999990494860951, 0.0416635772644784, -0.0013853657929132671, 2.3153011971441464e-05)


def _reduced(angle):
    turns = jnp.round(angle * INV_PI)
    for part in PI_PARTS:
        angle = angle - turns * part
    return angle


def _series(square, terms):
    total = square * terms[-1] + terms[-2]
    for term in terms[-3::-1]:
        total = total * square + term
    return total


def _snake(values, alpha, inverse):
    angle = _reduced(alpha * values)
    sine = angle * _series(angle * angle, SIN_TERMS)
    return values + sine * sine * inverse


def _snake_and_slope(values, alpha, inverse):
    angle = _reduced(alpha * values)
    square = angle * angle
    sine = angle * _series(square, SIN_TERMS)
    cosine = _series(square, COS_TERMS)
    return values + sine * sine * inverse, 1.0 + 2.0 * sine * cosine


def _dot(left, right):
    return jnp.dot(left, right, preferred_element_type=F32)


def _dot_nt(left, right):
    return lax.dot_general(left, right, (((1,), (1,)), ((), ())), preferred_element_type=F32)


def _dot_tn(left, right):
    return lax.dot_general(left, right, (((0,), (0,)), ((), ())), preferred_element_type=F32)


def _turn():
    count = GROUP * TILE_FRAMES
    target = lax.broadcasted_iota(jnp.int32, (count, count), 0)
    source = lax.broadcasted_iota(jnp.int32, (count, count), 1)
    wanted = (target % GROUP) * TILE_FRAMES + target // GROUP
    return jnp.where(source == wanted, 1.0, 0.0).astype(BF16)


def _teacher_act_kernel(place, tiles, alpha, keep, send):
    fsdp = place[2]
    turn = _turn()
    for out, first in ((keep, fsdp), (send, fsdp ^ 1)):
        for index in range(2):
            lanes = pl.ds(pl.multiple_of((first ^ (2 * index)) * QUARTER, QUARTER), QUARTER)
            scale = alpha[:, lanes]
            acted = _snake(_dot(turn, tiles[:, lanes]), scale, 1.0 / scale).astype(BF16)
            out[index] = acted.reshape(TILE_FRAMES, GROUP, QUARTER)


def _teacher_act(place, tiles, alpha):
    steps = TILE_DEV // GROUP
    shape = jax.ShapeDtypeStruct((2, TILE_FRAMES, TILE_DEV, QUARTER), BF16)
    return pl.pallas_call(
        _teacher_act_kernel,
        grid=(steps,),
        in_specs=[
            pl.BlockSpec(memory_space=pltpu.SMEM),
            pl.BlockSpec((GROUP * TILE_FRAMES, CT), lambda i: (i, 0)),
            pl.BlockSpec((1, CT), lambda i: (0, 0)),
        ],
        out_specs=[pl.BlockSpec((2, TILE_FRAMES, GROUP, QUARTER), lambda i: (0, 0, i, 0))] * 2,
        out_shape=[shape] * 2,
        name="teacher_act",
        compiler_params=pltpu.CompilerParams(vmem_limit_bytes=VMEM_LIMIT),
        cost_estimate=COST,
    )(place, tiles.reshape(ROWS, CT), alpha.reshape(1, CT))


def _pack_kernel(place, dilated, mix, down, proj, teacher, packed, early, late, sems):
    core, slab = place[0], place[3]
    copies = []
    row = 0
    for name, source in (("dilated", dilated), ("mix", mix), ("down", down), ("proj", proj)):
        rows = PACK[name]
        for block in range(PACK_COLS[name]):
            begin = pl.multiple_of((core * PACK_COLS[name] + block) * 128, 128)
            copies.append(pltpu.make_async_copy(
                source.at[pl.ds(pl.multiple_of(slab * rows, 16), rows), pl.ds(begin, 128)],
                packed.at[pl.ds(row, rows), :],
                sems.at[len(copies)],
            ))
            row += rows
    begin = pl.multiple_of((core * SLABS + slab) * 128, 128)
    half = KS * QUARTER // 2
    for index, out in enumerate((early, late)):
        source = teacher.at[index * half : (index + 1) * half, pl.ds(begin, 128)]
        copies.append(pltpu.make_async_copy(source, out, sems.at[len(copies)]))
    for copy in copies:
        copy.start()
    for copy in copies:
        copy.wait()


def _pack(place, *kernels):
    anywhere = pl.BlockSpec(memory_space=pl.ANY)
    return pl.pallas_call(
        _pack_kernel,
        in_specs=[pl.BlockSpec(memory_space=pltpu.SMEM)] + [anywhere] * 5,
        out_specs=[pl.BlockSpec(memory_space=pltpu.VMEM)] * 3,
        out_shape=[
            jax.ShapeDtypeStruct((PACK_ROWS, 128), BF16),
            jax.ShapeDtypeStruct((KS * QUARTER // 2, 128), BF16),
            jax.ShapeDtypeStruct((KS * QUARTER // 2, 128), BF16),
        ],
        scratch_shapes=[pltpu.SemaphoreType.DMA((10,))],
        name="pack_kernels",
        cost_estimate=COST,
    )(place, *kernels)


def _early(parts, slab):
    return parts[slab // 2].at[slab % 2]


def _late(parts, slab):
    return parts[2 + slab % 2].at[slab // 2]


def _windows(mine, theirs, quarter, offset):
    first = max(0, STRIDE * offset - MARGIN)
    wide = [
        jnp.concatenate([tiles[quarter, first + step] for step in range(STRIDE + MARGIN)], axis=1)
        for tiles in (mine, theirs)
    ]
    return jnp.concatenate(wide, axis=0), first - (STRIDE * offset - MARGIN)


def _teacher_near_kernel(mine, theirs, kernel, out):
    for offset in range(OUTF):
        wide, tap = _windows(mine, theirs, 0, offset)
        part = _dot(wide, kernel[tap * QUARTER : (tap + STRIDE + MARGIN) * QUARTER, :])
        for device in range(2):
            start = device * LATENTS + offset * TILE_DEV
            out[start : start + TILE_DEV, :] = part[device * TILE_DEV : (device + 1) * TILE_DEV, :]


def _teacher_near(mine, theirs, kernel):
    return pl.pallas_call(
        _teacher_near_kernel,
        out_shape=jax.ShapeDtypeStruct((2 * LATENTS, DL), F32),
        name="teacher_near",
        compiler_params=pltpu.CompilerParams(vmem_limit_bytes=WHOLE_VMEM),
        cost_estimate=COST,
    )(mine, theirs, kernel)


def _teacher_far_kernel(place, near, mine, theirs, *refs):
    own, other, (keep, send) = refs[:4], refs[4:8], refs[8:]
    core, plane = place[0], place[3]
    taps = KS // 2 * QUARTER
    skipped = MARGIN * QUARTER
    for offset in range(OUTF):
        wide, tap = _windows(mine, theirs, 1, offset)
        for side, source in enumerate((own, other)):
            for pair in range(0, SLABS, 2):
                columns = []
                for slab in (pair, pair + 1):
                    early, late = _early(source, slab)[...], _late(source, slab)[...]
                    if tap:
                        columns.append(jnp.concatenate([early[skipped:], late], axis=0))
                    else:
                        columns.append(jnp.concatenate([early, late[: taps - skipped]], axis=0))
                part = _dot(wide, jnp.concatenate(columns, axis=1))
                for index, slab in enumerate((pair, pair + 1)):
                    block = (core ^ side) * SLABS + (plane ^ slab)
                    lanes = pl.ds(pl.multiple_of(block * 128, 128), 128)
                    for device, out in enumerate((keep, send)):
                        piece = part[device * TILE_DEV : (device + 1) * TILE_DEV, index * 128 : (index + 1) * 128]
                        start = device * LATENTS + offset * TILE_DEV
                        piece += near[start : start + TILE_DEV, lanes]
                        out[offset * TILE_DEV : (offset + 1) * TILE_DEV, lanes] = piece.astype(out.dtype)


def _teacher_far(place, near, mine, theirs, own, other):
    whole = pl.BlockSpec(memory_space=pltpu.VMEM)
    return pl.pallas_call(
        _teacher_far_kernel,
        in_specs=[pl.BlockSpec(memory_space=pltpu.SMEM)] + [whole] * 11,
        out_specs=[whole] * 2,
        out_shape=[jax.ShapeDtypeStruct((LATENTS, DL), F32), jax.ShapeDtypeStruct((LATENTS, DL), BF16)],
        name="teacher_far",
        compiler_params=pltpu.CompilerParams(vmem_limit_bytes=WHOLE_VMEM),
        cost_estimate=COST,
    )(place, near, mine, theirs, *own, *other)


def _lanes(blocks, rows):
    return jnp.concatenate([blocks[index, rows, :] for index in range(blocks.shape[0])], axis=1)


def _forward_kernel(
    place, tiles, own_a, own_b, own_c, own_d, other_a, other_b, other_c, other_d,
    near_dilated, near_mix, near_down, near_proj, alphas, routes,
    act_one, act_two, act_three, slope_two, slope_three, student, predicted, mix, down, proj, parcel,
    dilated, held,
):
    own, other = (own_a, own_b, own_c, own_d), (other_a, other_b, other_c, other_d)
    core, fsdp, plane = place[0], place[2], place[3]

    def rows_of(quarter, slab, share):
        return pl.ds(pl.multiple_of(quarter * (SLABS * share) + slab * share, 16), share)

    kinds = ((near_dilated, dilated), (near_mix, mix), (near_down, down), (near_proj, proj))
    for name, (source, target) in zip(PACK, kinds):
        rows = pl.ds(pl.multiple_of(fsdp * (SLABS * PACK[name]), 16), SLABS * PACK[name])
        for block in range(target.shape[0]):
            target[block, rows, :] = source[:, block * 128 : (block + 1) * 128]
    for flip, pieces in enumerate((own, other)):
        side = core ^ flip
        for slab in range(SLABS):
            for bit in range(1, N_FSDP):
                early, late = _early(pieces, slab).at[bit - 1], _late(pieces, slab).at[bit - 1]
                quarter, chip = fsdp ^ bit, plane ^ slab
                dilated[side, rows_of(quarter, chip, PACK["dilated"]), :] = early[0:112, :]
                mix[side, rows_of(quarter, chip, PACK["mix"]), :] = early[112:128, :]
                rows = rows_of(quarter, chip, PACK["down"])
                down[side * 2, rows, :] = early[128:384, :]
                down[side * 2 + 1, rows, :] = late[0:256, :]
                rows = rows_of(quarter, chip, PACK["proj"])
                for block in range(4):
                    proj[side * 4 + block, rows, :] = late[256 + block * 32 : 288 + block * 32, :]

    alpha_one, alpha_two, alpha_three = alphas[0:1, :], alphas[1:2, :], alphas[2:3, :]
    inverse_one, inverse_two, inverse_three = 1.0 / alpha_one, 1.0 / alpha_two, 1.0 / alpha_three
    turn = _turn()
    for step in range(TILE_DEV // GROUP):
        turned = _dot(turn, tiles[step * GROUP * TILE_FRAMES : (step + 1) * GROUP * TILE_FRAMES, :])
        shape = (TILE_FRAMES, GROUP, CS)
        held[:, step * GROUP : (step + 1) * GROUP, :] = turned.astype(BF16).reshape(shape)
        acted = _snake(turned, alpha_one, inverse_one).astype(BF16)
        act_one[:, step * GROUP : (step + 1) * GROUP, :] = acted.reshape(shape)

    half_taps = DILATED_TAPS // 2
    spans = []
    for frame in range(TILE_FRAMES):
        valid = [tap for tap in range(DILATED_TAPS) if 0 <= frame + UNIT_DILATION * (tap - half_taps) < TILE_FRAMES]
        span = (valid[0], valid[-1] + 1)
        if spans and spans[-1][2] == span:
            spans[-1][1] = frame + 1
        else:
            spans.append([frame, frame + 1, span])
    for start, stop, (low, high) in spans:
        wide = jnp.concatenate(
            [
                act_one[start + shift : stop + shift].reshape((stop - start) * TILE_DEV, CS)
                for shift in (UNIT_DILATION * (tap - half_taps) for tap in range(low, high))
            ],
            axis=1,
        )
        hidden = _dot(wide, _lanes(dilated, slice(low * CS, high * CS)))
        acted, slope = _snake_and_slope(hidden, alpha_two, inverse_two)
        shape = (stop - start, TILE_DEV, CS)
        acted = acted.astype(BF16)
        act_two[start:stop] = acted.reshape(shape)
        slope_two[start:stop] = slope.reshape(shape)
        residual = held[start:stop].reshape((stop - start) * TILE_DEV, CS).astype(F32) + _dot(acted, _lanes(mix, slice(None)))
        acted, slope = _snake_and_slope(residual, alpha_three, inverse_three)
        act_three[start:stop] = acted.astype(BF16).reshape(shape)
        slope_three[start:stop] = slope.reshape(shape)

    reach = STRIDE + MARGIN
    for offset in range(OUTF):
        first = max(0, STRIDE * offset - MARGIN)
        tap = first - (STRIDE * offset - MARGIN)
        wide = jnp.concatenate([act_three[first + step] for step in range(reach)], axis=1)
        part = _dot(wide, _lanes(down, slice(tap * CS, (tap + reach) * CS)))
        student[offset * TILE_DEV : (offset + 1) * TILE_DEV, :] = part.astype(BF16)
    pick = jnp.where(
        routes[...] == lax.broadcasted_iota(jnp.int32, (TILE_DEV, TILE_DEV), 1), 1.0, 0.0
    ).astype(BF16)
    for offset in range(OUTF):
        rows = slice(offset * TILE_DEV, (offset + 1) * TILE_DEV)
        part = _dot(student[rows, :], _lanes(proj, slice(None)))
        predicted[rows, :] = part
        picked = _dot(pick, part.astype(BF16)).astype(BF16)
        for block in range(DL // CS):
            row = WINDOW_ROWS + (offset * (DL // CS) + block) * SHARE
            for owner in range(8):
                parcel[owner, row : row + SHARE, :] = picked[
                    owner * SHARE : (owner + 1) * SHARE, block * CS : (block + 1) * CS
                ]
    for tap in range(KS):
        for offset in range(OUTF):
            frame = STRIDE * offset - MARGIN + tap
            row = (tap % 2 * OUTF + offset) * TILE_DEV
            if 0 <= frame < TILE_FRAMES:
                parcel[tap // 2, row : row + TILE_DEV, :] = act_three[frame]
            else:
                parcel[tap // 2, row : row + TILE_DEV, :] = jnp.zeros((TILE_DEV, CS), BF16)


def _forward(place, tiles, own, other, kernels, alphas, routes):
    frames = (TILE_FRAMES, TILE_DEV, CS)
    whole = pl.BlockSpec(memory_space=pltpu.VMEM)
    return pl.pallas_call(
        _forward_kernel,
        in_specs=[
            pl.BlockSpec(memory_space=pltpu.SMEM),
            whole,
        ]
        + [whole] * 14,
        out_specs=[whole] * 11,
        out_shape=[
            jax.ShapeDtypeStruct(frames, BF16),
            jax.ShapeDtypeStruct(frames, BF16),
            jax.ShapeDtypeStruct(frames, BF16),
            jax.ShapeDtypeStruct(frames, F32),
            jax.ShapeDtypeStruct(frames, F32),
            jax.ShapeDtypeStruct((LATENTS, CSO), BF16),
            jax.ShapeDtypeStruct((LATENTS, DL), F32),
            jax.ShapeDtypeStruct((CS // 128, CS, 128), BF16),
            jax.ShapeDtypeStruct((CSO // 128, KS * CS, 128), BF16),
            jax.ShapeDtypeStruct((DL // 128, CSO, 128), BF16),
            jax.ShapeDtypeStruct((8, PARCEL_ROWS, CS), BF16),
        ],
        scratch_shapes=[
            pltpu.VMEM((CS // 128, DILATED_TAPS * CS, 128), BF16),
            pltpu.VMEM(frames, BF16),
        ],
        name="student_forward",
        compiler_params=pltpu.CompilerParams(vmem_limit_bytes=WHOLE_VMEM),
        cost_estimate=COST,
    )(place, tiles.reshape(ROWS, CS), *own, *other, *kernels, alphas, routes)


def _stacked(values, columns):
    return jnp.concatenate(
        [values[:, start : start + columns] for start in range(0, values.shape[1], columns)], axis=0
    )


def _error_kernel(
    place, target_own, target_other, predicted, weights, student, proj, back_student, send, keep, error, grad_proj
):
    me = place[1]
    weight = weights[...] * (1.0 / LATENTS)
    for offset in range(OUTF):
        rows = slice(offset * TILE_DEV, (offset + 1) * TILE_DEV)
        target = target_own[rows, :] + target_other[rows, :].astype(F32)
        target = target.astype(BF16).astype(F32)
        error[rows, :] = (weight * (predicted[rows, :] - target)).astype(BF16)
    back = _dot_nt(error[...], _lanes(proj, slice(None))).astype(BF16)
    back_student[...] = back.reshape(OUTF, TILE_DEV, CSO)
    grad_proj[...] = _dot_tn(student[...], error[...])
    for spot in range(CHUNKS):
        share = grad_proj[pl.ds(pl.multiple_of((me ^ spot) * 16, 16), 16), :]
        out = send if (spot // 4) % 2 else keep
        out[(spot // 8 % 2) * 8 + (spot // 16) * 4 + spot % 4] = _stacked(share, 256).astype(out.dtype)


def _error(place, targets, predicted, weights, student, proj):
    half = (CHUNKS // 2, 64, 256)
    whole = pl.BlockSpec(memory_space=pltpu.VMEM)
    return pl.pallas_call(
        _error_kernel,
        in_specs=[pl.BlockSpec(memory_space=pltpu.SMEM)] + [whole] * 6,
        out_specs=[whole] * 3,
        out_shape=[
            jax.ShapeDtypeStruct((OUTF, TILE_DEV, CSO), BF16),
            jax.ShapeDtypeStruct(half, BF16),
            jax.ShapeDtypeStruct(half, F32),
        ],
        scratch_shapes=[pltpu.VMEM((LATENTS, DL), BF16), pltpu.VMEM((CSO, DL), F32)],
        name="error_backward",
        compiler_params=pltpu.CompilerParams(vmem_limit_bytes=WHOLE_VMEM),
        cost_estimate=COST,
    )(place, *targets, predicted, weights, student, proj)


def _down_kernel(place, parcels, *refs):
    own, other, (keep, *sends), grads = refs[:4], refs[4:8], refs[8:12], refs[12]
    fsdp, chip = place[2], place[4]
    back = []
    for source in (own, other):
        for slab in range(SLABS):
            back += [_early(source, slab)[...], _late(source, slab)[...]]
    back = jnp.concatenate(back, axis=0)
    for tap in range(2):
        rows = []
        for side in range(2):
            for slab in range(SLABS):
                rows.append(parcels[chip ^ (2 * slab + side), tap * LATENTS : (tap + 1) * LATENTS, :])
        grads[tap * CS : (tap + 1) * CS, :] = _dot_tn(jnp.concatenate(rows, axis=0), back)
    for spot, out in enumerate((keep, *sends)):
        part = grads[pl.ds(pl.multiple_of((spot ^ fsdp) * 128, 128), 128), :]
        out[...] = part.astype(out.dtype)


def _down(place, parcels, own, other):
    whole = pl.BlockSpec(memory_space=pltpu.VMEM)
    return pl.pallas_call(
        _down_kernel,
        in_specs=[pl.BlockSpec(memory_space=pltpu.SMEM)] + [whole] * 9,
        out_specs=[whole] * 4,
        out_shape=[jax.ShapeDtypeStruct((128, CSO), F32)] + [jax.ShapeDtypeStruct((128, CSO), BF16)] * 3,
        scratch_shapes=[pltpu.VMEM((CSO, CSO), F32)],
        name="down_gradient",
        compiler_params=pltpu.CompilerParams(vmem_limit_bytes=VMEM_LIMIT),
        cost_estimate=COST,
    )(place, parcels, *own, *other)


def _flat(out, values):
    blocks = values.shape[1] // 128
    for block in range(blocks):
        out[pl.ds(block, values.shape[0], stride=blocks), :] = values[:, block * 128 : (block + 1) * 128]


def _finish_kernel(down, rest_proj, rest_other, *refs):
    downs, rests, (dilated, mix, full_down, proj) = refs[:3], refs[3:6], refs[6:]
    total = down[...]
    for part in downs:
        total += part[...].astype(F32)
    _flat(full_down, total)
    total = jnp.concatenate([rest_proj[...], rest_other[...]], axis=0)
    for part in rests:
        total += part[...].astype(F32)
    _flat(proj, jnp.concatenate([total[16 * i : 16 * (i + 1)] for i in range(4)], axis=1))
    _flat(dilated, total[64:120])
    _flat(mix, total[120:128])


def _finish(down, downs, rest, rests):
    whole = pl.BlockSpec(memory_space=pltpu.VMEM)
    return pl.pallas_call(
        _finish_kernel,
        in_specs=[whole] * 9,
        out_specs=[whole] * 4,
        out_shape=[jax.ShapeDtypeStruct((rows, 128), F32) for rows in (112, 16, 512, 128)],
        name="finish_gradients",
        compiler_params=pltpu.CompilerParams(vmem_limit_bytes=VMEM_LIMIT),
        cost_estimate=COST,
    )(down, *rest, *downs, *rests)


def _residual_kernel(
    place, back_student, down, mix, act_one, act_two, slope_two, slope_three,
    send, keep, back_three, back_residual, back_hidden, grad_dilated, grad_mix,
):
    me = place[1]
    back = back_student[...].reshape(LATENTS, CSO)
    for tap in range(KS):
        part = _dot_nt(back, _lanes(down, slice(tap * CS, (tap + 1) * CS)))
        for offset in range(OUTF):
            frame = STRIDE * offset - MARGIN + tap
            if 0 <= frame < TILE_FRAMES:
                piece = part[offset * TILE_DEV : (offset + 1) * TILE_DEV, :]
                if offset == 0 and frame >= MARGIN:
                    back_three[frame] += piece
                else:
                    back_three[frame] = piece
    for frame in range(0, TILE_FRAMES, 2):
        rows = slice(frame * TILE_DEV, (frame + 2) * TILE_DEV)
        shape = (2 * TILE_DEV, CS)
        share = back_three[frame : frame + 2].reshape(shape) * slope_three[frame : frame + 2].reshape(shape)
        share = share.astype(BF16)
        back_residual[rows, :] = share
        share = _dot_nt(share, _lanes(mix, slice(None))) * slope_two[frame : frame + 2].reshape(shape)
        back_hidden[rows, :] = share.astype(BF16)
    grad_mix[...] = _dot_tn(act_two[...].reshape(ROWS, CS), back_residual[...])
    half_taps = DILATED_TAPS // 2
    for tap in range(DILATED_TAPS):
        shift = UNIT_DILATION * (tap - half_taps)
        first, last = max(0, -shift), min(TILE_FRAMES, TILE_FRAMES - shift)
        rows = (last - first) * TILE_DEV
        grad_dilated[tap * CS : (tap + 1) * CS, :] = _dot_tn(
            act_one[first + shift : last + shift].reshape(rows, CS), back_hidden[first * TILE_DEV : last * TILE_DEV, :]
        )
    for place_index in range(CHUNKS):
        chunk = me ^ place_index
        part = jnp.concatenate(
            [
                grad_dilated[pl.ds(pl.multiple_of(chunk * 56, 8), 56), :],
                grad_mix[pl.ds(pl.multiple_of(chunk * 8, 8), 8), :],
            ],
            axis=0,
        )
        out = send if (place_index // 4) % 2 else keep
        out[(place_index // 8) * 4 + place_index % 4] = part.astype(out.dtype)


def _residual(place, back_student, down, mix, act_one, act_two, slope_two, slope_three):
    whole = pl.BlockSpec(memory_space=pltpu.VMEM)
    half = (CHUNKS // 2, 64, 256)
    return pl.pallas_call(
        _residual_kernel,
        in_specs=[pl.BlockSpec(memory_space=pltpu.SMEM)] + [whole] * 7,
        out_specs=[whole] * 2,
        out_shape=[jax.ShapeDtypeStruct(half, BF16), jax.ShapeDtypeStruct(half, F32)],
        scratch_shapes=[
            pltpu.VMEM((TILE_FRAMES, TILE_DEV, CS), F32),
            pltpu.VMEM((ROWS, CS), BF16),
            pltpu.VMEM((ROWS, CS), BF16),
            pltpu.VMEM((DILATED_TAPS * CS, CS), F32),
            pltpu.VMEM((CS, CS), F32),
        ],
        name="residual_backward",
        compiler_params=pltpu.CompilerParams(vmem_limit_bytes=WHOLE_VMEM),
        cost_estimate=COST,
    )(place, back_student, down, mix, act_one, act_two, slope_two, slope_three)


def _swap(values, axis, bit):
    return lax.ppermute(values, axis, [(i, i ^ bit) for i in range(lax.axis_size(axis))])


def on_device(
    student_tiles,
    teacher_tiles,
    send_list,
    clip_weight,
    kernel_dilated,
    kernel_mix,
    kernel_down,
    kernel_proj,
    kernel_teacher,
    alpha_one,
    alpha_two,
    alpha_three,
    alpha_teacher,
):
    n_dp = lax.axis_size("dp")
    d, f = lax.axis_index("dp"), lax.axis_index("fsdp")
    core, slab = d % 2, (d // 2) % SLABS
    halving = n_dp == 8
    me = d * N_FSDP + f if halving else jnp.int32(0)
    place = jnp.stack([core, me, f, slab, d % 8]).astype(jnp.int32)

    def plane_spread(early, late):
        return jnp.stack([early, _swap(early, "dp", 2)]), jnp.stack([late, _swap(late, "dp", 4)])

    def plane_gather(early, late):
        return early, _swap(early, "dp", 4), late, _swap(late, "dp", 2)

    def core_gather(own):
        return own, tuple(_swap(part, "dp", 1) for part in own)

    kernels = (kernel_dilated, kernel_mix, kernel_down, kernel_proj)
    flat_teacher = kernel_teacher.reshape(KS * QUARTER, DL)
    packed, early, late = _pack(place, *kernels, flat_teacher)
    fetched = [_swap(packed, "fsdp", bit) for bit in range(1, N_FSDP)]
    early, late = _swap(early, "fsdp", 2), _swap(late, "fsdp", 2)

    routes = send_list.reshape(-1)
    slot_weights = lax.all_to_all(
        clip_weight.reshape(n_dp, TILE_DEV // n_dp), "dp", split_axis=0, concat_axis=0, tiled=True
    ).reshape(-1)
    hits = routes[:, None] == jnp.arange(TILE_DEV, dtype=jnp.int32)[None, :]
    weights = jnp.sum(jnp.where(hits, slot_weights[:, None], 0.0), axis=0)[:, None]

    mine, sent = _teacher_act(place, teacher_tiles, alpha_teacher)
    fetched, sent, weights = lax.optimization_barrier((fetched, sent, weights))
    theirs = _swap(sent, "fsdp", 1)

    half = PACK_ROWS // 2
    spread = plane_spread(
        jnp.stack([part[:half] for part in fetched]), jnp.stack([part[half:] for part in fetched])
    )
    spread, early = lax.optimization_barrier((spread, early))
    own, other = core_gather(plane_gather(*spread))
    early, late, _ = lax.optimization_barrier((early, late, own))
    spread = plane_spread(early, late)
    teacher_own = plane_gather(*spread)
    own, other, _ = lax.optimization_barrier((own, other, spread))

    alphas = jnp.stack([alpha_one, alpha_two, alpha_three])
    (
        act_one, act_two, act_three, slope_two, slope_three, student, predicted, mix, down, proj, parcel,
    ) = _forward(place, student_tiles, own, other, kernels, alphas, routes[:, None])
    theirs, teacher_own, predicted = lax.optimization_barrier((theirs, teacher_own, predicted))
    teacher_own, teacher_other = core_gather(teacher_own)
    near = _teacher_near(mine, theirs, flat_teacher)
    target, partial = _teacher_far(place, near, mine, theirs, teacher_own, teacher_other)
    targets = (target, _swap(partial, "fsdp", 1))

    latent_rows = parcel[:, WINDOW_ROWS:].reshape(8, OUTF * DL // CS, SHARE, CS)
    if halving:
        parcels = lax.all_to_all(parcel, "dp", split_axis=0, concat_axis=0, tiled=True)
        latent = parcels[:, WINDOW_ROWS:].reshape(8, OUTF * DL // CS, SHARE, CS).transpose(0, 2, 1, 3)
    else:
        latent = latent_rows.transpose(0, 2, 1, 3).reshape(TILE_DEV, OUTF * DL)
        latent = lax.all_to_all(latent, "dp", split_axis=0, concat_axis=0, tiled=True)
    latent = latent.reshape(TILE_DEV, OUTF, DL)
    back_student, send_a, keep_a = _error(place, targets, predicted, weights, student, proj)
    send_b, keep_b = _residual(place, back_student, down, mix, act_one, act_two, slope_two, slope_three)

    if halving:
        def reduce_plane(send, keep, order):
            keep = keep.reshape(2, 2, N_FSDP, 64, 256)
            received = _swap(send, "dp", 1).reshape(keep.shape)
            for bit in (2, 4) if order == "xy" else (4, 2):
                keep, out = keep[0] + received[0].astype(F32), (keep[1] + received[1].astype(F32)).astype(BF16)
                received = _swap(out, "dp", bit)
            return keep + received.astype(F32)

        back_student, parcels = lax.optimization_barrier((back_student, parcels))
        keep_d, *sends = _down(place, parcels, *core_gather(plane_gather(*plane_spread(back_student[0], back_student[1]))))
        downs = [_swap(out, "fsdp", bit) for bit, out in zip(range(1, N_FSDP), sends)]
        rest_a, rest_b = reduce_plane(send_a, keep_a, "xy"), reduce_plane(send_b, keep_b, "yx")
        rest = jnp.concatenate([rest_a, rest_b], axis=1)
        rests = [_swap(rest[bit].astype(BF16), "fsdp", bit) for bit in range(1, N_FSDP)]
        grads = _finish(keep_d, downs, (rest_a[0], rest_b[0]), rests)
        grad_dilated, grad_mix, grad_down, grad_proj = [grad.reshape(-1) for grad in grads]
    else:
        def joined(send, keep):
            rows = keep.shape[-2]
            both = jnp.stack([keep.reshape(4, 4, rows, 256), send.astype(F32).reshape(4, 4, rows, 256)], axis=1)
            return both.reshape(CHUNKS, rows, 256)

        def scattered(values):
            return lax.psum_scatter(values.reshape(-1), ("dp", "fsdp"), scatter_dimension=0, tiled=True)

        turned = [jnp.swapaxes(half.reshape(2, 2, N_FSDP, 64, 256), 0, 1) for half in (send_a, keep_a)]
        part = jnp.concatenate([joined(*turned), joined(send_b, keep_b)], axis=1)
        windows = parcel[:, :WINDOW_ROWS].reshape(KS, OUTF, TILE_DEV, CS)
        grad_down = scattered(jnp.einsum("kotc,otd->kcd", windows, back_student, preferred_element_type=F32))
        grad_proj = scattered(jnp.concatenate([part[:, 16 * i : 16 * (i + 1)] for i in range(4)], axis=2))
        grad_dilated, grad_mix = scattered(part[:, 64:120]), scattered(part[:, 120:])
    return latent, grad_dilated, grad_mix, grad_down, grad_proj


def solution(mesh):
    placed = (
        P(("dp", "fsdp"), None, None),
        P(("dp", "fsdp"), None, None),
        P("dp", "fsdp", None),
        P(("dp", "fsdp")),
        P("fsdp", None),
        P("fsdp", None),
        P("fsdp", None),
        P("fsdp", None),
        P(None, "fsdp", None),
        P(),
        P(),
        P(),
        P(),
    )
    return jax.shard_map(
        on_device,
        mesh=mesh,
        in_specs=placed,
        out_specs=(
            P(("dp", "fsdp"), None, None),
            P(("dp", "fsdp")),
            P(("dp", "fsdp")),
            P(("dp", "fsdp")),
            P(("dp", "fsdp")),
        ),
        check_vma=False,
    )
```
